128 devices in a mesh: blk: 32 (over x, y, core), grp: 4 (over z).
Axes of the slice: x: 4, y: 4, z: 4, core: 2. Of those that a mesh axis runs over, the one named last changes fastest.
Arguments:
- populations: bfloat16 [1024, 19, 32, 1024], P(('blk', 'grp')), may hold values from 0.59765625 to 1.3984375
- solute: float32 [1024, 32, 1024], P(('blk', 'grp')), may hold values from 0 to 2
- solid_fraction: float32 [1024, 32, 1024], P(('blk', 'grp')), may hold values from 0.05 to 0.95
- neighbours: int32 [1024, 6], P(('blk', 'grp')), may hold values from 0 to 1023, as said below
- front_list: int32 [384], P(('blk', 'grp')), may hold values from 0 to 1023, as said below
- redeal_list: int32 [384], P(('blk', 'grp')), may hold values from 0 to 1023, as said below
Outputs:
- new_populations: bfloat16 [1024, 19, 32, 1024], P(('blk', 'grp'))
- new_solute: float32 [1024, 32, 1024], P(('blk', 'grp'))
- new_solid: float32 [1024, 32, 1024], P(('blk', 'grp'))
The draws below stay inside these ranges and needn't reach their ends.
Inputs may be any that keep to these rules, and one draw needn't show every extreme that they name: `neighbours`: the lists are symmetric: a block is the -x neighbour of its +x neighbour, and likewise for y and z. Every neighbour lies on another device with the same grp index. For each of the three directions, at most 1 block of one device have a neighbour in that direction (across either face) on any one other device, and some pair of devices reaches 1. `front_list`: the 3 entries stored on a device name distinct blocks of that device. Each device sends exactly one of its front blocks to each other device with the same blk index; every target is a block of the receiving device's front_list entries, each reached exactly once, so redeal_list is a permutation of front_list.
All inputs are finite; a program needn't handle non-finite values.
Results may differ from the reference program's by a relative error of at most 0.001.
Values may be sent and summed in bfloat16 or wider, within the bound.
A program may use at most 192 MiB of HBM per device.

```python
import jax
import jax.numpy as jnp
from jax import lax

S = 32
B_DEV = 8
NBLK = 1024
N_BLK = 32
N_GRP = 4


def shuffled_rows(key, row_count, length):
    return jax.vmap(lambda subkey: jax.random.permutation(subkey, length))(jax.random.split(key, row_count)).astype(jnp.int32)


def draw_neighbours(key, part):
    line_len = N_BLK
    group_len = N_GRP
    per_device = B_DEV
    offset_span = line_len // 2 - 1
    group_ids = jnp.arange(group_len, dtype=jnp.int32)[:, None, None]
    line_ids = jnp.arange(line_len, dtype=jnp.int32)[None, :, None]
    columns = []
    for axis_id in range(3):
        axis_key = jax.random.fold_in(key, axis_id)
        key_order, key_out, key_in = jax.random.split(axis_key, 3)
        line_order = shuffled_rows(key_order, group_len, line_len)
        line_place = jnp.argsort(line_order, axis=1).astype(jnp.int32)
        outward = shuffled_rows(key_out, group_len * line_len, per_device).reshape(group_len, line_len, per_device)
        inward = shuffled_rows(key_in, group_len * line_len, per_device).reshape(group_len, line_len, per_device)
        outward_inv = jnp.argsort(outward, axis=2).astype(jnp.int32)
        inward_inv = jnp.argsort(inward, axis=2).astype(jnp.int32)
        position_now = line_place[group_ids, line_ids]
        shift_up = 1 + outward % offset_span
        dest_line = line_order[group_ids, (position_now + shift_up) % line_len]
        dest_slot = inward[group_ids, dest_line, outward]
        upper_nbr = (dest_line * group_len + group_ids) * per_device + dest_slot
        shift_down = 1 + inward_inv % offset_span
        source_line = line_order[group_ids, (position_now - shift_down) % line_len]
        source_slot = outward_inv[group_ids, source_line, inward_inv]
        lower_nbr = (source_line * group_len + group_ids) * per_device + source_slot
        columns.append(jnp.transpose(lower_nbr, (1, 0, 2)).reshape(-1))
        columns.append(jnp.transpose(upper_nbr, (1, 0, 2)).reshape(-1))
    return jnp.stack(columns, axis=1).astype(jnp.int32)


def front_plan(key):
    base_key = jax.random.fold_in(key, 7)
    key_slots, key_out, key_in = jax.random.split(base_key, 3)
    devices_all = N_BLK * N_GRP
    moves_each = N_GRP - 1
    slot_order = shuffled_rows(key_slots, devices_all, B_DEV)[:, :moves_each]
    out_order = shuffled_rows(key_out, devices_all, moves_each)
    in_order = shuffled_rows(key_in, devices_all, moves_each)
    device_ids = jnp.arange(devices_all, dtype=jnp.int32)[:, None]
    line_ids = device_ids // N_GRP
    group_ids = device_ids % N_GRP
    dest_device = line_ids * N_GRP + (group_ids + 1 + out_order) % N_GRP
    entry_in = in_order[dest_device, out_order]
    dest_global = dest_device * B_DEV + slot_order[dest_device, entry_in]
    front_global = device_ids * B_DEV + slot_order
    return (front_global.reshape(-1).astype(jnp.int32), dest_global.reshape(-1).astype(jnp.int32))


def draw_front_list(key, part):
    return front_plan(key)[0]


def draw_redeal_list(key, part):
    return front_plan(key)[1]


def block_scale(rng, shape, cuts, least, high):
    def one(axis_at, parts):
        heights = jax.random.uniform(jax.random.fold_in(jax.random.fold_in(rng, 6), axis_at), (parts,), jnp.float32, least / len(cuts), high / len(cuts))
        return jnp.repeat(jnp.exp(heights), shape[axis_at] // parts).reshape((-1,) + (1,) * (len(shape) - axis_at - 1))

    loudness = one(*cuts[0])
    for cut in cuts[1:]:
        loudness = loudness * one(*cut)
    return loudness


def setup_inputs(seed: int = 0) -> dict:
    seeds = jax.random.split(jax.random.key(seed), 7)
    populations = jnp.clip(0.59765625 + 0.80078125 * jax.random.uniform(seeds[0], (NBLK, 19, S, S * S), jnp.float32) ** block_scale(seeds[0], (NBLK, 19, S, S * S), ((0, 128),), -0.2, 0.2), 0.59765625, 1.3984375).astype(jnp.bfloat16)
    solute = jnp.clip(2.0 * jax.random.uniform(seeds[1], (NBLK, S, S * S), jnp.float32) ** block_scale(seeds[1], (NBLK, S, S * S), ((0, 128),), -0.2, 0.2), 0.0, 2.0)
    solid_fraction = jnp.clip(0.05 + 0.9 * jax.random.uniform(seeds[2], (NBLK, S, S * S), jnp.float32) ** block_scale(seeds[2], (NBLK, S, S * S), ((0, 128),), -0.2, 0.2), 0.05, 0.95)
    neighbours = draw_neighbours(jax.random.fold_in(seeds[6], 71), 0)
    front_list = draw_front_list(jax.random.fold_in(seeds[6], 71), 0)
    redeal_list = draw_redeal_list(jax.random.fold_in(seeds[6], 71), 0)
    return {"populations": populations, "solute": solute, "solid_fraction": solid_fraction, "neighbours": neighbours, "front_list": front_list, "redeal_list": redeal_list}


VELOCITY = ((0, 0, 0), (1, 0, 0), (-1, 0, 0), (0, 1, 0), (0, -1, 0), (0, 0, 1), (0, 0, -1),
            (1, 1, 0), (-1, -1, 0), (1, -1, 0), (-1, 1, 0), (1, 0, 1), (-1, 0, -1), (1, 0, -1),
            (-1, 0, 1), (0, 1, 1), (0, -1, -1), (0, 1, -1), (0, -1, 1))
WEIGHTS = (1.0 / 3.0,) + (1.0 / 18.0,) * 6 + (1.0 / 36.0,) * 12
OPPOSITE = (0, 2, 1, 4, 3, 6, 5, 8, 7, 10, 9, 12, 11, 14, 13, 16, 15, 18, 17)
PLUS_X = (1, 7, 9, 11, 13)
MINUS_X = (2, 8, 10, 12, 14)
PLUS_Y = (3, 7, 10, 15, 17)
MINUS_Y = (4, 8, 9, 16, 18)
PLUS_Z = (5, 11, 14, 15, 18)
MINUS_Z = (6, 12, 13, 16, 17)
relax_time = 0.8
diffusivity = 0.1
rate_const = 0.5
saturation = 1.0


def face_planes(populations, solute, chosen_plus, chosen_minus, axis_id):
    block_count, velocities, extent, cell_count = populations.shape
    cube_view = populations.reshape(block_count, velocities, extent, extent, extent)
    solute_cube = solute.reshape(block_count, extent, extent, extent)
    top_index = extent - 1
    if axis_id == 0:
        upper_face, lower_face = cube_view[:, :, top_index], cube_view[:, :, 0]
        solute_upper, solute_lower = solute_cube[:, top_index], solute_cube[:, 0]
    elif axis_id == 1:
        upper_face, lower_face = cube_view[:, :, :, top_index], cube_view[:, :, :, 0]
        solute_upper, solute_lower = solute_cube[:, :, top_index], solute_cube[:, :, 0]
    else:
        upper_face, lower_face = cube_view[..., top_index], cube_view[..., 0]
        solute_upper, solute_lower = solute_cube[..., top_index], solute_cube[..., 0]
    upper_face = jnp.stack([upper_face[:, member] for member in chosen_plus], axis=1)
    lower_face = jnp.stack([lower_face[:, member] for member in chosen_minus], axis=1)
    return (upper_face.reshape(block_count, len(chosen_plus), cell_count),
            lower_face.reshape(block_count, len(chosen_minus), cell_count),
            solute_upper.reshape(block_count, cell_count),
            solute_lower.reshape(block_count, cell_count))


def edges_y(ghost_xlo, ghost_xhi, extent):
    block_count = ghost_xlo.shape[0]
    lower_view = ghost_xlo.reshape(block_count, 5, extent, extent)
    upper_view = ghost_xhi.reshape(block_count, 5, extent, extent)
    top_index = extent - 1
    rows_upper = jnp.stack([lower_view[:, 1, top_index], upper_view[:, 2, top_index]], axis=1)
    rows_lower = jnp.stack([lower_view[:, 2, 0], upper_view[:, 1, 0]], axis=1)
    return rows_upper, rows_lower


def edges_z(ghost_xlo, ghost_xhi, ghost_ylo, ghost_yhi, extent):
    block_count = ghost_xlo.shape[0]
    xlo_view = ghost_xlo.reshape(block_count, 5, extent, extent)
    xhi_view = ghost_xhi.reshape(block_count, 5, extent, extent)
    ylo_view = ghost_ylo.reshape(block_count, 5, extent, extent)
    yhi_view = ghost_yhi.reshape(block_count, 5, extent, extent)
    top_index = extent - 1
    rows_upper = jnp.stack([xlo_view[:, 3, :, top_index], xhi_view[:, 4, :, top_index],
                            ylo_view[:, 3, :, top_index], yhi_view[:, 4, :, top_index]], axis=1)
    rows_lower = jnp.stack([xlo_view[:, 4, :, 0], xhi_view[:, 3, :, 0],
                            ylo_view[:, 4, :, 0], yhi_view[:, 3, :, 0]], axis=1)
    return rows_upper, rows_lower


def pull_one(populations, ghosts, direction, extent):
    ghost_xlo, ghost_xhi, ghost_ylo, ghost_yhi, rows_ylo, rows_yhi, ghost_zlo, ghost_zhi, rows_zlo, rows_zhi = ghosts
    step_x, step_y, step_z = VELOCITY[direction]
    block_count = populations.shape[0]
    shifted = populations[:, direction]
    if step_x == 1:
        shifted = jnp.concatenate([ghost_xlo[:, PLUS_X.index(direction)][:, None], shifted[:, :-1]], axis=1)
    if step_x == -1:
        shifted = jnp.concatenate([shifted[:, 1:], ghost_xhi[:, MINUS_X.index(direction)][:, None]], axis=1)
    if step_y != 0:
        if step_y == 1:
            face_plane = ghost_ylo[:, PLUS_Y.index(direction)]
            edge_rows = rows_ylo
        else:
            face_plane = ghost_yhi[:, MINUS_Y.index(direction)]
            edge_rows = rows_yhi
        face_plane = face_plane.reshape(block_count, extent, extent)
        if step_x == 1:
            face_plane = jnp.concatenate([edge_rows[:, 0][:, None], face_plane[:, :-1]], axis=1)
        if step_x == -1:
            face_plane = jnp.concatenate([face_plane[:, 1:], edge_rows[:, 1][:, None]], axis=1)
        if step_y == 1:
            shifted = jnp.concatenate([face_plane, shifted[:, :, :-extent]], axis=2)
        else:
            shifted = jnp.concatenate([shifted[:, :, extent:], face_plane], axis=2)
    if step_z != 0:
        if step_z == 1:
            face_plane = ghost_zlo[:, PLUS_Z.index(direction)]
            edge_rows = rows_zlo
        else:
            face_plane = ghost_zhi[:, MINUS_Z.index(direction)]
            edge_rows = rows_zhi
        face_plane = face_plane.reshape(block_count, extent, extent)
        if step_x == 1:
            face_plane = jnp.concatenate([edge_rows[:, 0][:, None], face_plane[:, :-1]], axis=1)
        if step_x == -1:
            face_plane = jnp.concatenate([face_plane[:, 1:], edge_rows[:, 1][:, None]], axis=1)
        if step_y == 1:
            face_plane = jnp.concatenate([edge_rows[:, 2][:, :, None], face_plane[:, :, :-1]], axis=2)
        if step_y == -1:
            face_plane = jnp.concatenate([face_plane[:, :, 1:], edge_rows[:, 3][:, :, None]], axis=2)
        spread = jnp.repeat(face_plane, extent, axis=2)
        depth_pos = lax.broadcasted_iota(jnp.int32, shifted.shape, 2) % extent
        if step_z == 1:
            shifted = jnp.where(depth_pos == 0, spread, jnp.roll(shifted, 1, axis=2))
        else:
            shifted = jnp.where(depth_pos == extent - 1, spread, jnp.roll(shifted, -1, axis=2))
    return shifted


def local_update(populations, solute, solid_fraction, ghosts, solute_ghosts):
    block_count, velocities, extent, cell_count = populations.shape
    pulled = [pull_one(populations, ghosts, direction, extent) for direction in range(19)]
    widened = [member.astype(jnp.float32) for member in pulled]
    density = jnp.zeros(solute.shape, jnp.float32)
    moment_x = jnp.zeros(solute.shape, jnp.float32)
    moment_y = jnp.zeros(solute.shape, jnp.float32)
    moment_z = jnp.zeros(solute.shape, jnp.float32)
    for direction in range(19):
        weighted = WEIGHTS[direction] * widened[direction]
        density = density + weighted
        step_x, step_y, step_z = VELOCITY[direction]
        if step_x != 0:
            moment_x = moment_x + step_x * weighted
        if step_y != 0:
            moment_y = moment_y + step_y * weighted
        if step_z != 0:
            moment_z = moment_z + step_z * weighted
    speed_x = moment_x / density
    speed_y = moment_y / density
    speed_z = moment_z / density
    speed_sq = speed_x * speed_x + speed_y * speed_y + speed_z * speed_z
    keep_share = 1.0 - solid_fraction
    collided = []
    for direction in range(19):
        step_x, step_y, step_z = VELOCITY[direction]
        along = step_x * speed_x + step_y * speed_y + step_z * speed_z
        equilibrium = density * (1.0 + 3.0 * along + 4.5 * along * along - 1.5 * speed_sq)
        current = widened[direction]
        relaxed = keep_share * (current + (equilibrium - current) / relax_time) + solid_fraction * widened[OPPOSITE[direction]]
        collided.append(relaxed.astype(jnp.bfloat16))
    new_populations = jnp.stack(collided, axis=1)
    solute_xlo, solute_xhi, solute_ylo, solute_yhi, solute_zlo, solute_zhi = solute_ghosts
    below_x = jnp.concatenate([solute_xlo[:, None], solute[:, :-1]], axis=1)
    above_x = jnp.concatenate([solute[:, 1:], solute_xhi[:, None]], axis=1)
    below_y = jnp.concatenate([solute_ylo.reshape(block_count, extent, extent), solute[:, :, :-extent]], axis=2)
    above_y = jnp.concatenate([solute[:, :, extent:], solute_yhi.reshape(block_count, extent, extent)], axis=2)
    depth_pos = lax.broadcasted_iota(jnp.int32, solute.shape, 2) % extent
    below_z = jnp.where(depth_pos == 0, jnp.repeat(solute_zlo.reshape(block_count, extent, extent), extent, axis=2),
                        jnp.roll(solute, 1, axis=2))
    above_z = jnp.where(depth_pos == extent - 1, jnp.repeat(solute_zhi.reshape(block_count, extent, extent), extent, axis=2),
                        jnp.roll(solute, -1, axis=2))
    laplace = below_x + above_x + below_y + above_y + below_z + above_z - 6.0 * solute
    advect = 0.5 * (speed_x * (above_x - below_x) + speed_y * (above_y - below_y) + speed_z * (above_z - below_z))
    mixed = solute + diffusivity * laplace - advect
    reaction = rate_const * solid_fraction * (1.0 - solid_fraction) * (saturation - mixed)
    return new_populations, mixed + reaction, solid_fraction - reaction


def reference(populations, solute, solid_fraction, neighbours, front_list, redeal_list):
    extent = S
    upper_x, lower_x, sol_upper_x, sol_lower_x = face_planes(populations, solute, PLUS_X, MINUS_X, 0)
    ghost_xlo = jnp.take(upper_x, neighbours[:, 0], axis=0)
    ghost_xhi = jnp.take(lower_x, neighbours[:, 1], axis=0)
    solute_xlo = jnp.take(sol_upper_x, neighbours[:, 0], axis=0)
    solute_xhi = jnp.take(sol_lower_x, neighbours[:, 1], axis=0)
    upper_y, lower_y, sol_upper_y, sol_lower_y = face_planes(populations, solute, PLUS_Y, MINUS_Y, 1)
    rows_upper_y, rows_lower_y = edges_y(ghost_xlo, ghost_xhi, extent)
    ghost_ylo = jnp.take(upper_y, neighbours[:, 2], axis=0)
    ghost_yhi = jnp.take(lower_y, neighbours[:, 3], axis=0)
    rows_ylo = jnp.take(rows_upper_y, neighbours[:, 2], axis=0)
    rows_yhi = jnp.take(rows_lower_y, neighbours[:, 3], axis=0)
    solute_ylo = jnp.take(sol_upper_y, neighbours[:, 2], axis=0)
    solute_yhi = jnp.take(sol_lower_y, neighbours[:, 3], axis=0)
    upper_z, lower_z, sol_upper_z, sol_lower_z = face_planes(populations, solute, PLUS_Z, MINUS_Z, 2)
    rows_upper_z, rows_lower_z = edges_z(ghost_xlo, ghost_xhi, ghost_ylo, ghost_yhi, extent)
    ghost_zlo = jnp.take(upper_z, neighbours[:, 4], axis=0)
    ghost_zhi = jnp.take(lower_z, neighbours[:, 5], axis=0)
    rows_zlo = jnp.take(rows_upper_z, neighbours[:, 4], axis=0)
    rows_zhi = jnp.take(rows_lower_z, neighbours[:, 5], axis=0)
    solute_zlo = jnp.take(sol_upper_z, neighbours[:, 4], axis=0)
    solute_zhi = jnp.take(sol_lower_z, neighbours[:, 5], axis=0)
    everything = (populations, solute, solid_fraction,
                  ghost_xlo, ghost_xhi, ghost_ylo, ghost_yhi, rows_ylo, rows_yhi,
                  ghost_zlo, ghost_zhi, rows_zlo, rows_zhi,
                  solute_xlo, solute_xhi, solute_ylo, solute_yhi, solute_zlo, solute_zhi)
    group_size = 8
    grouped = tuple(member_arr.reshape((NBLK // group_size, group_size) + member_arr.shape[1:]) for member_arr in everything)

    def run_group(batch_items):
        return local_update(batch_items[0], batch_items[1], batch_items[2], batch_items[3:13], batch_items[13:19])

    collided, reacted, dissolved = lax.map(run_group, grouped)
    collided = collided.reshape(populations.shape)
    reacted = reacted.reshape(solute.shape)
    dissolved = dissolved.reshape(solid_fraction.shape)
    new_populations = collided.at[redeal_list].set(jnp.ones((redeal_list.shape[0],) + populations.shape[1:], jnp.bfloat16))
    new_solute = reacted.at[redeal_list].set(jnp.take(reacted, front_list, axis=0))
    new_solid = dissolved.at[redeal_list].set(jnp.take(dissolved, front_list, axis=0))
    return new_populations, new_solute, new_solid
```

```python
import jax
import jax.numpy as jnp
from jax import lax
from jax.experimental import pallas as pl
from jax.experimental.pallas import tpu as pltpu
from jax.sharding import PartitionSpec as P

VELOCITY = (
    (0, 0, 0), (1, 0, 0), (-1, 0, 0), (0, 1, 0), (0, -1, 0), (0, 0, 1), (0, 0, -1),
    (1, 1, 0), (-1, -1, 0), (1, -1, 0), (-1, 1, 0), (1, 0, 1), (-1, 0, -1), (1, 0, -1),
    (-1, 0, 1), (0, 1, 1), (0, -1, -1), (0, 1, -1), (0, -1, 1),
)
LEAVES = (
    ((2, 8, 10, 12, 14), (1, 7, 9, 11, 13)),
    ((4, 8, 9, 16, 18), (3, 7, 10, 15, 17)),
    ((6, 12, 13, 16, 17), (5, 11, 14, 15, 18)),
)
FETCH = (6, 12, 13, 16, 17, 5, 11, 14, 15, 18, 4, 8, 9, 3, 7, 10, 2, 1)
SLOTS = 8
S = 32
CELLS = S * S
PEERS = 32
GROUPS = 4
F32, BF16, I32 = jnp.float32, jnp.bfloat16, jnp.int32
relax_time = 0.8
diffusivity = 0.1
rate_const = 0.5
saturation = 1.0


def iota(shape, dim):
    return lax.broadcasted_iota(I32, shape, dim)


def dot(a, b):
    return jnp.dot(a, b, preferred_element_type=F32)


def exchange_kernel(pop_hbm, sol_ref, nbr, inv, redeal, gx_ref, gy_ref, gz_ref, table_ref,
                    pop, fx, fy, fz, sa, sb, se, ra, rb, re, ex, mine, fetch_sem, send_sem, recv_sem,
                    table_send, table_recv):
    me = lax.axis_index("blk")
    grp = lax.axis_index("grp")

    def fetch(direction):
        return pltpu.make_async_copy(pop_hbm.at[:, direction], pop.at[direction], fetch_sem.at[direction])

    for direction in FETCH:
        fetch(direction).start()

    barrier = pltpu.get_barrier_semaphore()

    @pl.loop(1, PEERS)
    def _(k):
        pl.semaphore_signal(barrier, inc=1, device_id={"blk": (me + k) % PEERS}, device_id_type=pl.DeviceIdType.MESH)

    for k in range(1, GROUPS):
        pl.semaphore_signal(barrier, inc=1, device_id={"grp": (grp + k) % GROUPS}, device_id_type=pl.DeviceIdType.MESH)

    lane_of = iota((8, 128), 1)
    mine[...] = jnp.where(lane_of == 0, redeal[0], jnp.where(lane_of == 1, redeal[1], redeal[2]))

    deep, lane = iota((CELLS, 128), 0), iota((CELLS, 128), 1) % S
    pick = [jnp.where(deep == lane * S + z, 1.0, 0.0).astype(BF16) for z in (0, S - 1)]
    wide, lane = iota((128, 128), 0), iota((128, 128), 1) % S
    pick_y = [jnp.where(wide == lane + first, 1.0, 0.0).astype(BF16) for first in (0, 128 - S)]
    quarter = iota((SLOTS * S, 128), 1) // S

    def spread_items(parts, later):
        low = jnp.where(quarter == 0, parts[0], jnp.where(quarter == 1, parts[1], jnp.where(quarter == 2, parts[2], parts[3])))
        high = jnp.where(quarter == later, parts[4], parts[5])
        return low.reshape(SLOTS, S, 128).astype(BF16), high.reshape(SLOTS, S, 128).astype(BF16)

    fetched = set()

    def ready(directions):
        for direction in directions:
            if direction not in fetched:
                fetched.add(direction)
                fetch(direction).wait()

    sol = sol_ref[...].reshape(SLOTS * S, CELLS).astype(BF16)
    for side in range(2):
        ready(LEAVES[2][side])
        parts = [dot(pop[d].reshape(SLOTS * S, CELLS), pick[side]) for d in LEAVES[2][side]] + [dot(sol, pick[side])]
        low, high = spread_items(parts, 2)
        fz[:, side, :, 0:128] = low
        fz[:, side, :, 128:256] = high
    for side in range(2):
        ready(LEAVES[1][side])
        at = slice(CELLS - 128, CELLS) if side else slice(0, 128)
        parts = [dot(pop[d, :, :, at].reshape(SLOTS * S, 128), pick_y[side]) for d in LEAVES[1][side]]
        parts.append(dot(sol[:, at], pick_y[side]))
        low, high = spread_items(parts, 0)
        fy[:, side, :, 0:128] = low
        fy[:, side, :, 128:256] = high
    for side in range(2):
        ready(LEAVES[0][side])

        @pl.loop(0, SLOTS)
        def _(slot):
            if side:
                rows = [pop[d, slot, 16:32, :].astype(F32)[15:16] for d in LEAVES[0][side]]
                rows.append(sol_ref[slot, 31:32, :])
            else:
                rows = [pop[d, slot, 0:16, :].astype(F32)[0:1] for d in LEAVES[0][side]]
                rows.append(sol_ref[slot, 0:1, :])
            rows.append(jnp.zeros((2, CELLS), F32))
            rows = jnp.concatenate(rows, axis=0)
            fx[slot, side] = jnp.concatenate([rows[:, :512], rows[:, 512:]], axis=0).astype(BF16)

    pl.semaphore_wait(barrier, PEERS - 1 + GROUPS - 1)

    def send(src, dst, which, peer):
        return pltpu.make_async_remote_copy(
            src_ref=src.at[peer], dst_ref=dst.at[me], send_sem=send_sem.at[which], recv_sem=recv_sem.at[which],
            device_id={"blk": peer}, device_id_type=pl.DeviceIdType.MESH)

    def all_of(src, dst, which):
        return pltpu.make_async_remote_copy(
            src_ref=src.at[pl.ds(0, PEERS - 1)], dst_ref=dst.at[pl.ds(0, PEERS - 1)], send_sem=send_sem.at[which],
            recv_sem=recv_sem.at[which], device_id={"blk": (me + 1) % PEERS}, device_id_type=pl.DeviceIdType.MESH)

    def table_copy(k):
        return pltpu.make_async_remote_copy(
            src_ref=mine, dst_ref=table_ref.at[grp], send_sem=table_send.at[k], recv_sem=table_recv.at[k],
            device_id={"grp": (grp + k) % GROUPS}, device_id_type=pl.DeviceIdType.MESH)

    left = iota((S, 128), 1) < 64

    @pl.loop(1, PEERS)
    def _(k):
        peer = (me + k) % PEERS
        at_x, at_y, at_z = inv[0, peer], inv[1, peer], inv[2, peer]
        y_part = fy[at_y // 2, at_y % 2]
        z_part = fz[at_z // 2, at_z % 2]
        mixed = jnp.where(left, y_part[:, 128:].astype(F32), z_part[:, 128:].astype(F32)).astype(BF16)
        sa[peer, :, 0:512] = fx[at_x // 2, at_x % 2]
        sa[peer, :, 512:640] = y_part[0:16, 0:128]
        sa[peer, :, 640:768] = mixed[0:16]
        sa[peer, :, 768:896] = y_part[16:32, 0:128]
        sa[peer, :, 896:1024] = mixed[16:32]
        sb[peer] = z_part[:, 0:128]
        send(sa, ra, 0, peer).start()

    @pl.loop(1, PEERS)
    def _(k):
        send(sb, rb, 1, (me + k) % PEERS).start()

    for k in range(1, GROUPS):
        table_copy(k).start()

    all_of(sa, ra, 0).wait_recv()

    def owner(slot, face):
        return nbr[slot, face] // (SLOTS * GROUPS)

    @pl.loop(0, SLOTS)
    def _(slot):
        halves = []
        for side in range(2):
            part = ra[owner(slot, side), :, 0:512].astype(F32)
            halves.append(jnp.concatenate([part[0:8], part[8:16]], axis=1))
        gx_ref[slot] = jnp.concatenate(halves, axis=0).astype(BF16)
        for side in range(2):
            peer = owner(slot, 2 + side)
            gy_ref[slot, side, 0:16, :] = ra[peer, :, 512:768]
            gy_ref[slot, side, 16:32, :] = ra[peer, :, 768:1024]

    ghosts = gx_ref[...].reshape(SLOTS * 16, CELLS)
    ex[0] = dot(ghosts, pick[0]).reshape(SLOTS, 16, 128)
    ex[1] = dot(ghosts, pick[1]).reshape(SLOTS, 16, 128)
    ex[2] = dot(ghosts[:, 0:128], pick_y[0]).reshape(SLOTS, 16, 128)
    ex[3] = dot(ghosts[:, CELLS - 128:], pick_y[1]).reshape(SLOTS, 16, 128)
    row32, lane32 = iota((S, 128), 0), iota((S, 128), 1)
    first = lane32[0:1] < 64

    @pl.loop(0, SLOTS)
    def _(slot):
        y_lo = gy_ref[slot, 0].astype(F32)
        y_hi = gy_ref[slot, 1].astype(F32)
        for side in range(2):
            if side:
                y_row = jnp.where(first, ex[3, slot, 1:2], ex[3, slot, 10:11])
                z_row = jnp.where(first, ex[1, slot, 3:4], ex[1, slot, 12:13])
                third, fourth = y_lo[:, 127:128], y_hi[:, 159:160]
            else:
                y_row = jnp.where(first, ex[2, slot, 9:10], ex[2, slot, 2:3])
                z_row = jnp.where(first, ex[0, slot, 11:12], ex[0, slot, 4:5])
                third, fourth = y_hi[:, 96:97], y_lo[:, 128:129]
            cols = jnp.where(lane32 == 96, third, fourth)
            fy[slot, side, :, 0:128] = jnp.broadcast_to(y_row, (S, 128)).astype(BF16)
            fz[slot, side, :, 0:128] = jnp.where(lane32 < 96, z_row, cols).astype(BF16)

    top = (row32 < 16) & (lane32 < 96)

    @pl.loop(1, PEERS)
    def _(k):
        peer = (me + k) % PEERS
        at_y, at_z = inv[1, peer], inv[2, peer]
        se[peer] = jnp.where(top, fy[at_y // 2, at_y % 2, :, 0:128].astype(F32),
                             fz[at_z // 2, at_z % 2, :, 0:128].astype(F32)).astype(BF16)
        send(se, re, 2, peer).start()

    all_of(sb, rb, 1).wait_recv()
    all_of(se, re, 2).wait_recv()
    item = lane32 // S
    lane = lane32 % S

    @pl.loop(0, SLOTS)
    def _(slot):
        for side in range(2):
            down, up = (1, 2) if side == 0 else (2, 1)
            edge = re[owner(slot, 2 + side), 0:16, :].astype(F32)[0:1]
            plane = gy_ref[slot, side, :, 0:128].astype(F32)
            plane = jnp.where(item == down, jnp.concatenate([edge, plane[:S - 1]], axis=0),
                              jnp.where(item == up, jnp.concatenate([plane[1:], edge], axis=0), plane))
            gy_ref[slot, side, :, 0:128] = plane.astype(BF16)
            peer = owner(slot, 4 + side)
            edges = re[peer].astype(F32)
            edge = edges[16:17]
            plane = rb[peer].astype(F32)
            late = jnp.concatenate([ra[peer, :, 640:768], ra[peer, :, 896:1024]], axis=0).astype(F32)
            third, fourth = edges[:, 96:97], edges[:, 97:98]
            if side == 0:
                moved = jnp.where(lane == 0, third, pltpu.roll(plane, 1, 1))
                moved_late = jnp.where(lane == S - 1, fourth, pltpu.roll(late, 127, 1))
            else:
                moved = jnp.where(lane == S - 1, third, pltpu.roll(plane, 127, 1))
                moved_late = jnp.where(lane == 0, fourth, pltpu.roll(late, 1, 1))
            plane = jnp.where(item == down, jnp.concatenate([edge, plane[:S - 1]], axis=0),
                              jnp.where(item == up, jnp.concatenate([plane[1:], edge], axis=0),
                                        jnp.where(item == 3, moved, plane)))
            gz_ref[slot, side, :, 0:128] = plane.astype(BF16)
            gz_ref[slot, side, :, 128:256] = jnp.where(item == 2, moved_late, late).astype(BF16)

    all_of(sa, ra, 0).wait_send()
    all_of(sb, rb, 1).wait_send()
    all_of(se, re, 2).wait_send()
    for k in range(1, GROUPS):
        table_copy(k).wait()


def exchange(populations, solute, neighbours, inverse, redeal_list):
    vmem, smem, anywhere = (pl.BlockSpec(memory_space=m) for m in (pltpu.VMEM, pltpu.SMEM, pl.ANY))
    return pl.pallas_call(
        exchange_kernel,
        out_shape=(
            jax.ShapeDtypeStruct((SLOTS, 16, CELLS), BF16),
            jax.ShapeDtypeStruct((SLOTS, 2, S, 256), BF16),
            jax.ShapeDtypeStruct((SLOTS, 2, S, 256), BF16),
            jax.ShapeDtypeStruct((GROUPS, 8, 128), I32),
        ),
        in_specs=[anywhere, vmem, smem, smem, smem],
        out_specs=(vmem, vmem, vmem, vmem),
        scratch_shapes=[
            pltpu.VMEM((19, SLOTS, S, CELLS), BF16),
            pltpu.VMEM((SLOTS, 2, 16, 512), BF16),
            pltpu.VMEM((SLOTS, 2, S, 256), BF16),
            pltpu.VMEM((SLOTS, 2, S, 256), BF16),
            pltpu.VMEM((PEERS, 16, 1024), BF16),
            pltpu.VMEM((PEERS, S, 128), BF16),
            pltpu.VMEM((PEERS, S, 128), BF16),
            pltpu.VMEM((PEERS, 16, 1024), BF16),
            pltpu.VMEM((PEERS, S, 128), BF16),
            pltpu.VMEM((PEERS, S, 128), BF16),
            pltpu.VMEM((4, SLOTS, 16, 128), F32),
            pltpu.VMEM((8, 128), I32),
            pltpu.SemaphoreType.DMA((19,)),
            pltpu.SemaphoreType.DMA((3,)),
            pltpu.SemaphoreType.DMA((3,)),
            pltpu.SemaphoreType.DMA((GROUPS,)),
            pltpu.SemaphoreType.DMA((GROUPS,)),
        ],
        compiler_params=pltpu.CompilerParams(collective_id=0, has_side_effects=True, vmem_limit_bytes=48 * 2**20),
        cost_estimate=pl.CostEstimate(flops=10**9, bytes_accessed=12 * 10**6, transcendentals=0),
        name="exchange",
    )(populations, solute, neighbours, inverse, redeal_list)


def pull_block(pop, sol, gx, gy, gz, spread, pulled, grads):
    lane = iota((S, CELLS), 1)
    depth = lane % S
    lane128 = iota((S, 128), 1)
    part = lane128 // S
    x_rows = gx[...].astype(F32)
    y_tiles = [[gy[side, :, 128 * t:128 * t + 128].astype(F32) for t in range(2)] for side in range(2)]
    stack = []
    for side in range(2):
        for item in range(6):
            tile = gz[side, :, 0:128] if item < 4 else gz[side, :, 128:256]
            quarter = item if item < 4 else item - 2
            stack.append(jnp.where(part == quarter, tile.astype(F32), 0.0).astype(BF16))
    z_all = dot(jnp.concatenate(stack, axis=0), spread[...])

    def z_ghost(side, item):
        at = (side * 6 + item) * S
        return z_all[at:at + S]

    def y_merge(block, side, item, cz):
        tile = y_tiles[side][item // 4]
        start = (item % 4) * S
        target = 0 if side == 0 else 128 - S
        shift = (target + cz - start) % 128
        if shift:
            tile = pltpu.roll(tile, shift, 1)
        if side == 0:
            return jnp.concatenate([jnp.where(lane128 < S, tile, block[:, 0:128]), block[:, 128:]], axis=1)
        return jnp.concatenate([block[:, :CELLS - 128], jnp.where(lane128 >= 128 - S, tile, block[:, CELLS - 128:])], axis=1)

    def shift_x(block, side, item):
        row = x_rows[side * 8 + item:side * 8 + item + 1]
        if side == 0:
            return jnp.concatenate([row, block[:S - 1]], axis=0)
        return jnp.concatenate([block[1:], row], axis=0)

    for d, (cx, cy, cz) in enumerate(VELOCITY):
        block = pop[d].astype(F32)
        if cx:
            side = 0 if cx == 1 else 1
            block = shift_x(block, side, LEAVES[0][1 - side].index(d))
        shift = (S * cy + cz) % CELLS
        if shift:
            block = pltpu.roll(block, shift, 1)
        if cy:
            side = 0 if cy == 1 else 1
            block = y_merge(block, side, LEAVES[1][1 - side].index(d), cz)
        if cz:
            side = 0 if cz == 1 else 1
            edge = 0 if cz == 1 else S - 1
            block = jnp.where(depth == edge, z_ghost(side, LEAVES[2][1 - side].index(d)), block)
        pulled[d] = block
    here = sol[...]
    below, above = shift_x(here, 0, 5), shift_x(here, 1, 5)
    total = below + above
    grads[1] = above - below
    below = y_merge(pltpu.roll(here, S, 1), 0, 5, 0)
    above = y_merge(pltpu.roll(here, CELLS - S, 1), 1, 5, 0)
    total = total + below + above
    grads[2] = above - below
    below = jnp.where(depth == 0, z_ghost(0, 5), pltpu.roll(here, 1, 1))
    above = jnp.where(depth == S - 1, z_ghost(1, 5), pltpu.roll(here, CELLS - 1, 1))
    grads[3] = above - below
    grads[0] = total + below + above - 6.0 * here


def update(pulled, grads, sol, solid, rows, lanes, put):
    f = [pulled[d, rows, lanes] for d in range(19)]
    pair_sum = [f[i] + f[i + 1] for i in range(1, 19, 2)]
    pair_dif = [f[i] - f[i + 1] for i in range(1, 19, 2)]
    straight = pair_sum[0] + pair_sum[1] + pair_sum[2]
    slanted = (pair_sum[3] + pair_sum[4]) + (pair_sum[5] + pair_sum[6]) + (pair_sum[7] + pair_sum[8])
    density = f[0] * (1.0 / 3.0) + straight * (1.0 / 18.0) + slanted * (1.0 / 36.0)
    dif = pair_dif
    over = 1.0 / density
    over36 = over * (1.0 / 36.0)
    ux = (2.0 * dif[0] + ((dif[3] + dif[4]) + (dif[5] + dif[6]))) * over36
    uy = (2.0 * dif[1] + ((dif[3] - dif[4]) + (dif[7] + dif[8]))) * over36
    uz = (2.0 * dif[2] + ((dif[5] - dif[6]) + (dif[7] - dif[8]))) * over36
    amount = solid[rows, lanes]
    keep = 1.0 - amount
    if put is not None:
        scale = (1.0 / relax_time) * keep * density
        base = scale - (1.5 * scale) * (ux * ux + uy * uy + uz * uz)
        curve, slope = 4.5 * scale, 3.0 * scale
        rest = (1.0 / relax_time - 1.0) * keep
        even_part, odd_part = 0.5 * (amount - rest), 0.5 * (amount + rest)
        put(0, base + (amount - rest) * f[0])
        along_all = (ux, uy, uz, ux + uy, ux - uy, ux + uz, ux - uz, uy + uz, uy - uz)
        for pair in range(9):
            along = along_all[pair]
            even = base + (curve * along) * along + even_part * pair_sum[pair]
            odd = slope * along - odd_part * pair_dif[pair]
            put(2 * pair + 1, even + odd)
            put(2 * pair + 2, even - odd)
    mixed = (sol[rows, lanes] + diffusivity * grads[0, rows, lanes]
             - 0.5 * (ux * grads[1, rows, lanes] + uy * grads[2, rows, lanes] + uz * grads[3, rows, lanes]))
    reaction = rate_const * amount * keep * (saturation - mixed)
    return mixed + reaction, amount - reaction


def make_spread(spread):
    deep, lane = iota((128, CELLS), 0), iota((128, CELLS), 1)
    spread[...] = jnp.where(deep % S == lane // S, 1.0, 0.0).astype(BF16)


def chunks(body):
    @pl.loop(0, 16)
    def _(step):
        rows = pl.ds(pl.multiple_of((step // 8) * 16, 16), 16)
        lanes = pl.ds(pl.multiple_of((step % 8) * 128, 128), 128)
        body(rows, lanes)


def front_kernel(front, redeal, pop, sol, solid, gx, gy, gz, send1, send2, send3, ones_ref, spread, pulled, grads):
    step = pl.program_id(0)

    @pl.when(step == 0)
    def _():
        make_spread(spread)

    ones_ref[...] = jnp.ones(ones_ref.shape, BF16)
    pull_block(pop.at[0], sol.at[0], gx.at[0], gy.at[0], gz.at[0], spread, pulled, grads)
    for target, ref in enumerate((send1, send2, send3)):
        @pl.when(step == target)
        def _():
            def one(rows, lanes):
                ref[0, rows, lanes], ref[1, rows, lanes] = update(pulled, grads, sol.at[0], solid.at[0], rows, lanes, None)

            chunks(one)


def rest_kernel(front, pop, sol, solid, gx, gy, gz, old_ref, new_pop, new_sol, new_solid, spread, pulled, grads):
    @pl.when(pl.program_id(0) == 0)
    def _():
        make_spread(spread)

    pull_block(pop.at[0], sol.at[0], gx.at[0], gy.at[0], gz.at[0], spread, pulled, grads)

    def one(rows, lanes):
        def put(direction, value):
            new_pop[0, direction, rows, lanes] = value.astype(BF16)

        new_sol[0, rows, lanes], new_solid[0, rows, lanes] = update(
            pulled, grads, sol.at[0], solid.at[0], rows, lanes, put)

    chunks(one)


def front_slot(step, front, redeal):
    group = front[0] // SLOTS % GROUPS
    slot = front[0] % SLOTS
    for entry in range(1, 3):
        ahead = (redeal[entry] // SLOTS % GROUPS - group + GROUPS) % GROUPS
        slot = jnp.where(ahead == step + 1, front[entry] % SLOTS, slot)
    return slot


def rest_slot(step, front):
    a, b, c = (front[entry] % SLOTS for entry in range(3))
    low, high = jnp.minimum(a, b), jnp.maximum(a, b)
    mid, high = jnp.minimum(high, c), jnp.maximum(high, c)
    low, mid = jnp.minimum(low, mid), jnp.maximum(low, mid)
    slot = step
    for taken in (low, mid, high):
        slot = slot + jnp.where(slot >= taken, 1, 0)
    return slot


def block_specs(pick):
    shapes = ((1, 19, S, CELLS), (1, S, CELLS), (1, S, CELLS), (1, 16, CELLS), (1, 2, S, 256), (1, 2, S, 256))
    return [pl.BlockSpec(shape, lambda step, *refs, n=len(shape): (pick(step, *refs),) + (0,) * (n - 1)) for shape in shapes]


WORK = [
    pltpu.VMEM((128, CELLS), BF16),
    pltpu.VMEM((19, S, CELLS), F32),
    pltpu.VMEM((4, S, CELLS), F32),
]


def front_update(front, redeal, populations, solute, solid_fraction, gx, gy, gz):
    specs = block_specs(front_slot)
    sent = pl.BlockSpec((2, S, CELLS), lambda *_: (0, 0, 0))
    return pl.pallas_call(
        front_kernel,
        out_shape=tuple(jax.ShapeDtypeStruct((2, S, CELLS), F32) for _ in range(3))
        + (jax.ShapeDtypeStruct(populations.shape, BF16),),
        grid_spec=pltpu.PrefetchScalarGridSpec(
            num_scalar_prefetch=2, grid=(3,), in_specs=specs, out_specs=(sent, sent, sent, specs[0]),
            scratch_shapes=WORK),
        compiler_params=pltpu.CompilerParams(vmem_limit_bytes=40 * 2**20),
        cost_estimate=pl.CostEstimate(flops=2 * 10**7, bytes_accessed=9 * 10**6, transcendentals=0),
        name="front",
    )(front, redeal, populations, solute, solid_fraction, gx, gy, gz)


def rest_update(front, populations, solute, solid_fraction, gx, gy, gz, new_populations):
    specs = block_specs(rest_slot)
    return pl.pallas_call(
        rest_kernel,
        out_shape=(
            jax.ShapeDtypeStruct(populations.shape, BF16),
            jax.ShapeDtypeStruct(solute.shape, F32),
            jax.ShapeDtypeStruct(solute.shape, F32),
        ),
        grid_spec=pltpu.PrefetchScalarGridSpec(
            num_scalar_prefetch=1, grid=(5,), in_specs=specs + [pl.BlockSpec(memory_space=pl.ANY)],
            out_specs=tuple(specs[:3]), scratch_shapes=WORK),
        input_output_aliases={7: 0},
        compiler_params=pltpu.CompilerParams(vmem_limit_bytes=40 * 2**20),
        cost_estimate=pl.CostEstimate(flops=10**8, bytes_accessed=16 * 10**6, transcendentals=0),
        name="rest",
    )(front, populations, solute, solid_fraction, gx, gy, gz, new_populations)


def place_kernel(front, table, got1, got2, got3, old_sol, old_solid, new_sol, new_solid):
    for k, got in enumerate((got1, got2, got3)):
        @pl.when(pl.program_id(0) == k)
        def _():
            new_sol[0] = got[0]
            new_solid[0] = got[1]


def place_slot(step, front, table):
    group = front[0] // SLOTS % GROUPS
    source = (group + GROUPS - 1 - step) % GROUPS
    slot = table[source, 0] % SLOTS
    for entry in range(1, 3):
        place = table[source, entry]
        slot = jnp.where(place // SLOTS % GROUPS == group, place % SLOTS, slot)
    return slot


def place_front(front, table, received, new_solute, new_solid):
    whole = pl.BlockSpec((2, S, CELLS), lambda *_: (0, 0, 0))
    landed = pl.BlockSpec((1, S, CELLS), lambda *refs: (place_slot(*refs), 0, 0))
    anywhere = pl.BlockSpec(memory_space=pl.ANY)
    return pl.pallas_call(
        place_kernel,
        out_shape=tuple(jax.ShapeDtypeStruct(new_solute.shape, F32) for _ in range(2)),
        grid_spec=pltpu.PrefetchScalarGridSpec(
            num_scalar_prefetch=2, grid=(3,), in_specs=[whole] * 3 + [anywhere] * 2, out_specs=(landed, landed)),
        input_output_aliases={5: 0, 6: 1},
        cost_estimate=pl.CostEstimate(flops=0, bytes_accessed=2 * 10**6, transcendentals=0),
        name="place",
    )(front, table, *received, new_solute, new_solid)


def body(populations, solute, solid_fraction, neighbours, front_list, redeal_list):
    owner = (neighbours // (SLOTS * GROUPS)).reshape(SLOTS, 3, 2)
    face = 2 * jnp.arange(SLOTS, dtype=I32)[:, None, None] + jnp.arange(2, dtype=I32)[None, None, :]
    hits = owner[..., None] == jnp.arange(PEERS, dtype=I32)
    inverse = jnp.sum(jnp.where(hits, face[..., None], 0), axis=(0, 2), dtype=I32)
    gx, gy, gz, table = exchange(populations, solute, neighbours, inverse, redeal_list)
    *sent, new_populations = front_update(front_list, redeal_list, populations, solute, solid_fraction, gx, gy, gz)
    received = [
        lax.ppermute(sent[k], "grp", [(g, (g + k + 1) % GROUPS) for g in range(GROUPS)]) for k in range(GROUPS - 1)
    ]
    new_populations, new_solute, new_solid = rest_update(
        front_list, populations, solute, solid_fraction, gx, gy, gz, new_populations)
    new_solute, new_solid = place_front(front_list, table[:, 0, :8], received, new_solute, new_solid)
    return new_populations, new_solute, new_solid


def solution(mesh):
    deal = ("blk", "grp")
    return jax.shard_map(
        body,
        mesh=mesh,
        in_specs=(P(deal, None, None, None), P(deal, None, None), P(deal, None, None), P(deal, None), P(deal), P(deal)),
        out_specs=(P(deal, None, None, None), P(deal, None, None), P(deal, None, None)),
        check_vma=False,
    )
```

```python
import jax
import jax.numpy as jnp
from jax import lax
from jax.experimental import pallas as pl
from jax.experimental.pallas import tpu as pltpu
from jax.sharding import PartitionSpec as P

VELOCITY = (
    (0, 0, 0), (1, 0, 0), (-1, 0, 0), (0, 1, 0), (0, -1, 0), (0, 0, 1), (0, 0, -1),
    (1, 1, 0), (-1, -1, 0), (1, -1, 0), (-1, 1, 0), (1, 0, 1), (-1, 0, -1), (1, 0, -1),
    (-1, 0, 1), (0, 1, 1), (0, -1, -1), (0, 1, -1), (0, -1, 1),
)
LEAVES = (
    ((2, 8, 10, 12, 14), (1, 7, 9, 11, 13)),
    ((4, 8, 9, 16, 18), (3, 7, 10, 15, 17)),
    ((6, 12, 13, 16, 17), (5, 11, 14, 15, 18)),
)
FETCH = (2, 8, 10, 12, 14, 1, 7, 9, 11, 13, 15, 16, 17, 18, 3, 4, 6, 5)
SLOTS = 8
S = 32
CELLS = S * S
PEERS = 32
GROUPS = 4
F32, BF16, I32 = jnp.float32, jnp.bfloat16, jnp.int32
relax_time = 0.8
diffusivity = 0.1
rate_const = 0.5
saturation = 1.0


def iota(shape, dim):
    return lax.broadcasted_iota(I32, shape, dim)


def dot(a, b):
    return jnp.dot(a, b, preferred_element_type=F32)


def exchange_kernel(pop_hbm, sol_hbm, nbr_hbm, redeal_hbm, gx_ref, gy_ref, gz_ref, table_ref,
                    pop, sol_ref, xr, fx, fy, fz, lx, ly, ey, ez, s1, s2, s3, r1, r2, r3, mine, inv_vmem,
                    nbr, inv, redeal, fetch_sem, small_sem, send_sem, recv_sem, table_send, table_recv):
    me = lax.axis_index("blk")
    grp = lax.axis_index("grp")

    def fetch(direction):
        return pltpu.make_async_copy(pop_hbm.at[:, direction], pop.at[direction], fetch_sem.at[direction])

    nbr_copy = pltpu.make_async_copy(nbr_hbm, nbr, small_sem.at[0])
    redeal_copy = pltpu.make_async_copy(redeal_hbm, redeal, small_sem.at[1])
    inv_copy = pltpu.make_async_copy(inv_vmem, inv, small_sem.at[2])
    sol_copy = pltpu.make_async_copy(sol_hbm, sol_ref, small_sem.at[3])
    nbr_copy.start()
    redeal_copy.start()
    sol_copy.start()
    for direction in FETCH:
        fetch(direction).start()

    barrier = pltpu.get_barrier_semaphore()

    @pl.loop(1, PEERS)
    def _(k):
        pl.semaphore_signal(barrier, inc=1, device_id={"blk": (me + k) % PEERS}, device_id_type=pl.DeviceIdType.MESH)

    for k in range(1, GROUPS):
        pl.semaphore_signal(barrier, inc=1, device_id={"grp": (grp + k) % GROUPS}, device_id_type=pl.DeviceIdType.MESH)

    deep, lane = iota((CELLS, 128), 0), iota((CELLS, 128), 1) % S
    pick = [jnp.where(deep == lane * S + z, 1.0, 0.0).astype(BF16) for z in (0, S - 1)]
    wide, lane = iota((128, 128), 0), iota((128, 128), 1) % S
    pick_y = [jnp.where(wide == lane + first, 1.0, 0.0).astype(BF16) for first in (0, 128 - S)]

    nbr_copy.wait()
    redeal_copy.wait()

    def owner(slot, face):
        return nbr[slot, face] // (SLOTS * GROUPS)

    row8, lane8 = iota((8, 128), 0), iota((8, 128), 1)
    found = jnp.zeros((8, 128), I32)
    for axis in range(3):
        hit = jnp.zeros((8, 128), I32)
        for slot in range(SLOTS):
            for side in range(2):
                hit = jnp.where(lane8 == owner(slot, 2 * axis + side), 2 * slot + side, hit)
        found = jnp.where(row8 == axis, hit, found)
    inv_vmem[...] = found
    inv_copy.start()
    lane1 = iota((1, 128), 1)
    mine[...] = jnp.where(lane1 == 0, redeal[0], jnp.where(lane1 == 1, redeal[1], redeal[2]))
    sol_copy.wait()

    fetched = set()

    def ready(directions):
        for direction in directions:
            if direction not in fetched:
                fetched.add(direction)
                fetch(direction).wait()

    ready(LEAVES[0][0] + LEAVES[0][1])

    @pl.loop(0, SLOTS)
    def _(slot):
        faces = []
        for side in range(2):
            at, row = (16, 15) if side else (0, 0)
            rows = [pop[d, slot, at:at + 16, :].astype(F32)[row:row + 1] for d in LEAVES[0][side]]
            rows.append(sol_ref[slot, at + row:at + row + 1, :])
            rows.append(jnp.zeros((2, CELLS), F32))
            rows = jnp.concatenate(rows, axis=0)
            fx[2 * slot + side] = jnp.concatenate([rows[:, :512], rows[:, 512:]], axis=0).astype(BF16)
            faces.append(rows)
        xr[slot] = jnp.concatenate(faces, axis=0).astype(BF16)

    faces = xr[...].reshape(SLOTS * 16, CELLS)
    z_low, z_top = dot(faces, pick[0]), dot(faces, pick[1])
    y_low, y_top = dot(faces[:, 0:128], pick_y[0]), dot(faces[:, CELLS - 128:], pick_y[1])
    quarter1 = lane1 // S
    ready((15, 16, 17, 18))
    high = slice(CELLS - 128, CELLS)
    lane16 = iota((16, 128), 1)

    def across(d, at, z):
        one = jnp.where(lane16 == z, 1.0, 0.0).astype(BF16)
        tile = pop[d, :, :, at].reshape(SLOTS * S, 128)
        return lax.dot_general(one, tile, (((1,), (1,)), ((), ())), preferred_element_type=F32)

    y_lines = ((across(16, slice(0, 128), 0), across(18, slice(0, 128), S - 1)),
               (across(15, high, 127), across(17, high, 128 - S)))
    for slot in range(SLOTS):
        for side in range(2):
            row = slot * 16 + side * 8
            four = (y_top, y_low, z_top, z_low) if side else (y_low, y_top, z_low, z_top)
            four = [part[row + 1 + i:row + 2 + i] for i, part in enumerate(four)]
            line = jnp.where(quarter1 == 0, four[0], jnp.where(quarter1 == 1, four[1], jnp.where(quarter1 == 2, four[2], four[3])))
            lx[2 * slot + side] = jnp.broadcast_to(line, (16, 128)).astype(BF16)
            tiles = [part[:, 128 * (slot // 4):128 * (slot // 4) + 128] for part in y_lines[side]]
            shift = (128 - S * (slot % 4)) % 128
            if shift:
                tiles[0] = pltpu.roll(tiles[0], shift, 1)
            shift = (shift + S) % 128
            if shift:
                tiles[1] = pltpu.roll(tiles[1], shift, 1)
            ly[2 * slot + side] = jnp.where(lane16 < S, tiles[0], tiles[1]).astype(BF16)

    inv_copy.wait()
    pl.semaphore_wait(barrier, PEERS - 1 + GROUPS - 1)

    def send(src, dst, which, peer):
        return pltpu.make_async_remote_copy(
            src_ref=src.at[peer], dst_ref=dst.at[me], send_sem=send_sem.at[which], recv_sem=recv_sem.at[which],
            device_id={"blk": peer}, device_id_type=pl.DeviceIdType.MESH)

    def all_of(src, dst, which):
        return pltpu.make_async_remote_copy(
            src_ref=src.at[pl.ds(0, PEERS - 1)], dst_ref=dst.at[pl.ds(0, PEERS - 1)], send_sem=send_sem.at[which],
            recv_sem=recv_sem.at[which], device_id={"blk": (me + 1) % PEERS}, device_id_type=pl.DeviceIdType.MESH)

    def table_copy(k):
        return pltpu.make_async_remote_copy(
            src_ref=mine, dst_ref=table_ref.at[grp], send_sem=table_send.at[k], recv_sem=table_recv.at[k],
            device_id={"grp": (grp + k) % GROUPS}, device_id_type=pl.DeviceIdType.MESH)

    upper8 = iota((16, 128), 0) < 8

    @pl.loop(1, PEERS)
    def _(k):
        peer = (me + k) % PEERS
        s1[peer] = jnp.where(upper8, lx[inv[0, peer]].astype(F32), ly[inv[1, peer]].astype(F32)).astype(BF16)
        send(s1, r1, 0, peer).start()

    for k in range(1, GROUPS):
        table_copy(k).start()

    quarter = iota((SLOTS * S, 128), 1) // S

    def place_items(into, side, parts, later):
        low = jnp.where(quarter == 0, parts[0], jnp.where(quarter == 1, parts[1], jnp.where(quarter == 2, parts[2], parts[3])))
        late = jnp.where(quarter == later, parts[4], parts[5])
        low, late = low.reshape(SLOTS, S, 128).astype(BF16), late.reshape(SLOTS, S, 128).astype(BF16)
        for slot in range(SLOTS):
            into[2 * slot + side, :, 0:128] = low[slot]
            into[2 * slot + side, :, 128:256] = late[slot]

    sol = sol_ref[...].reshape(SLOTS * S, CELLS).astype(BF16)
    for side in range(2):
        ready(LEAVES[1][side])
        at = high if side else slice(0, 128)
        parts = [dot(pop[d, :, :, at].reshape(SLOTS * S, 128), pick_y[side]) for d in LEAVES[1][side]]
        parts.append(dot(sol[:, at], pick_y[side]))
        place_items(fy, side, parts, 0)
    for side in range(2):
        ready(LEAVES[2][side])
        parts = [dot(pop[d].reshape(SLOTS * S, CELLS), pick[side]) for d in LEAVES[2][side]] + [dot(sol, pick[side])]
        place_items(fz, side, parts, 2)

    left = iota((S, 128), 1) < 64

    @pl.loop(1, PEERS)
    def _(k):
        peer = (me + k) % PEERS
        y_part, z_part = fy[inv[1, peer]], fz[inv[2, peer]]
        s2[peer, :, 0:128] = y_part[:, 0:128]
        s2[peer, :, 128:256] = jnp.where(left, y_part[:, 128:].astype(F32), z_part[:, 128:].astype(F32)).astype(BF16)
        s2[peer, :, 256:384] = z_part[:, 0:128]
        send(s2, r2, 1, peer).start()

    all_of(s1, r1, 0).wait_recv()

    def lines(face, row):
        return jnp.concatenate([r1[owner(slot, face)].astype(F32)[row:row + 1] for slot in range(SLOTS)], axis=0)

    x_lo, x_hi, y_lo, y_hi = lines(0, 0), lines(1, 0), lines(2, 8), lines(3, 8)
    quarter8 = lane8 // S
    back = [pltpu.roll(part, 128 - S, 1) for part in (x_lo, x_hi, y_lo, y_hi)]
    x_lo, x_hi = pltpu.roll(x_lo, S, 1), pltpu.roll(x_hi, S, 1)

    def four_of(one, two, three, zero):
        return jnp.where(quarter8 == 1, one, jnp.where(quarter8 == 2, two, jnp.where(quarter8 == 3, three, zero)))

    y_rows = (jnp.where(quarter8 == 1, x_hi, x_lo), jnp.where(quarter8 == 1, x_lo, x_hi))
    z_rows = (four_of(back[1], back[0], back[3], back[2]), four_of(back[0], back[1], back[2], back[3]))
    for slot in range(SLOTS):
        for side in range(2):
            ey[2 * slot + side] = jnp.broadcast_to(y_rows[side][slot:slot + 1], (16, 128))
            ez[2 * slot + side] = jnp.broadcast_to(z_rows[side][slot:slot + 1], (16, 128))
    row16 = iota((16, 128), 0)

    @pl.loop(1, PEERS)
    def _(k):
        peer = (me + k) % PEERS
        part = fx[inv[0, peer]]
        first = jnp.where(row16 == 6, ey[inv[1, peer]], jnp.where(row16 == 7, ez[inv[2, peer]], part[:, 0:128].astype(F32)))
        s3[peer, :, 0:128] = first.astype(BF16)
        s3[peer, :, 128:512] = part[:, 128:512]
        send(s3, r3, 2, peer).start()

    all_of(s2, r2, 1).wait_recv()
    row32, lane32 = iota((S, 128), 0), iota((S, 128), 1)
    item = lane32 // S

    def shift_rows(plane, down, up):
        return jnp.where(item == down, pltpu.roll(plane, 1, 0), jnp.where(item == up, pltpu.roll(plane, S - 1, 0), plane))

    @pl.loop(0, SLOTS)
    def _(slot):
        for side in range(2):
            down, up = (1, 2) if side == 0 else (2, 1)
            peer = owner(slot, 2 + side)
            gy_ref[slot, side, :, 0:128] = shift_rows(r2[peer, :, 0:128].astype(F32), down, up).astype(BF16)
            gy_ref[slot, side, :, 128:256] = r2[peer, :, 128:256]
            peer = owner(slot, 4 + side)
            plane, late = r2[peer, :, 256:384].astype(F32), r2[peer, :, 128:256].astype(F32)
            turn = 1 if side == 0 else 127
            plane = jnp.where(item == 3, pltpu.roll(plane, turn, 1), shift_rows(plane, down, up))
            gz_ref[slot, side, :, 0:128] = plane.astype(BF16)
            gz_ref[slot, side, :, 128:256] = jnp.where(item == 2, pltpu.roll(late, 128 - turn, 1), late).astype(BF16)

    all_of(s3, r3, 2).wait_recv()

    @pl.loop(0, SLOTS)
    def _(slot):
        halves = []
        for side in range(2):
            part = r3[owner(slot, side)].astype(F32)
            halves.append(jnp.concatenate([part[0:8], part[8:16]], axis=1))
        gx_ref[slot] = jnp.concatenate(halves, axis=0).astype(BF16)
        for side in range(2):
            down, up = (1, 2) if side == 0 else (2, 1)
            ends = ((item == down) & (row32 == 0)) | ((item == up) & (row32 == S - 1))
            edge = r3[owner(slot, 2 + side), :, 0:128].astype(F32)[6:7]
            plane = gy_ref[slot, side, :, 0:128].astype(F32)
            gy_ref[slot, side, :, 0:128] = jnp.where(ends, edge, plane).astype(BF16)
            edge = r3[owner(slot, 4 + side), :, 0:128].astype(F32)[7:8]
            third = jnp.sum(jnp.where(lane32 == row32 + 96, edge, 0.0), axis=1, keepdims=True)
            fourth = jnp.sum(jnp.where(lane32 == row32, edge, 0.0), axis=1, keepdims=True)
            plane, late = gz_ref[slot, side, :, 0:128].astype(F32), gz_ref[slot, side, :, 128:256].astype(F32)
            at3, at4 = (96, 95) if side == 0 else (127, 64)
            gz_ref[slot, side, :, 0:128] = jnp.where(ends, edge, jnp.where(lane32 == at3, third, plane)).astype(BF16)
            gz_ref[slot, side, :, 128:256] = jnp.where(lane32 == at4, fourth, late).astype(BF16)

    all_of(s1, r1, 0).wait_send()
    all_of(s2, r2, 1).wait_send()
    all_of(s3, r3, 2).wait_send()
    for k in range(1, GROUPS):
        table_copy(k).wait()


def exchange(populations, solute, neighbours, redeal_list):
    vmem, hbm = (pl.BlockSpec(memory_space=m) for m in (pltpu.VMEM, pltpu.HBM))
    return pl.pallas_call(
        exchange_kernel,
        out_shape=(
            jax.ShapeDtypeStruct((SLOTS, 16, CELLS), BF16),
            jax.ShapeDtypeStruct((SLOTS, 2, S, 256), BF16),
            jax.ShapeDtypeStruct((SLOTS, 2, S, 256), BF16),
            jax.ShapeDtypeStruct((GROUPS, 1, 128), I32),
        ),
        in_specs=[hbm] * 4,
        out_specs=(vmem, vmem, vmem, vmem),
        scratch_shapes=[
            pltpu.VMEM((19, SLOTS, S, CELLS), BF16),
            pltpu.VMEM((SLOTS, S, CELLS), F32),
            pltpu.VMEM((SLOTS, 16, CELLS), BF16),
            pltpu.VMEM((2 * SLOTS, 16, 512), BF16),
            pltpu.VMEM((2 * SLOTS, S, 256), BF16),
            pltpu.VMEM((2 * SLOTS, S, 256), BF16),
            pltpu.VMEM((2 * SLOTS, 16, 128), BF16),
            pltpu.VMEM((2 * SLOTS, 16, 128), BF16),
            pltpu.VMEM((2 * SLOTS, 16, 128), F32),
            pltpu.VMEM((2 * SLOTS, 16, 128), F32),
            pltpu.VMEM((PEERS, 16, 128), BF16),
            pltpu.VMEM((PEERS, S, 384), BF16),
            pltpu.VMEM((PEERS, 16, 512), BF16),
            pltpu.VMEM((PEERS, 16, 128), BF16),
            pltpu.VMEM((PEERS, S, 384), BF16),
            pltpu.VMEM((PEERS, 16, 512), BF16),
            pltpu.VMEM((1, 128), I32),
            pltpu.VMEM((8, 128), I32),
            pltpu.SMEM((SLOTS, 6), I32),
            pltpu.SMEM((8, 128), I32),
            pltpu.SMEM((3,), I32),
            pltpu.SemaphoreType.DMA((19,)),
            pltpu.SemaphoreType.DMA((4,)),
            pltpu.SemaphoreType.DMA((3,)),
            pltpu.SemaphoreType.DMA((3,)),
            pltpu.SemaphoreType.DMA((GROUPS,)),
            pltpu.SemaphoreType.DMA((GROUPS,)),
        ],
        compiler_params=pltpu.CompilerParams(collective_id=0, has_side_effects=True, vmem_limit_bytes=28 * 2**20),
        cost_estimate=pl.CostEstimate(flops=10**9, bytes_accessed=12 * 10**6, transcendentals=0),
        name="exchange",
    )(*(pltpu.with_memory_space_constraint(a, pltpu.HBM) for a in (populations, solute, neighbours, redeal_list)))


def pull_block(pop, sol, gx, gy, gz, spread, pulled, grads):
    lane = iota((S, CELLS), 1)
    depth = lane % S
    lane128 = iota((S, 128), 1)
    part = lane128 // S
    x_rows = gx[...].astype(F32)
    y_tiles = [[gy[side, :, 128 * t:128 * t + 128].astype(F32) for t in range(2)] for side in range(2)]
    stack = []
    for side in range(2):
        for item in range(6):
            tile = gz[side, :, 0:128] if item < 4 else gz[side, :, 128:256]
            quarter = item if item < 4 else item - 2
            stack.append(jnp.where(part == quarter, tile.astype(F32), 0.0).astype(BF16))
    z_all = dot(jnp.concatenate(stack, axis=0), spread[...])

    def z_ghost(side, item):
        at = (side * 6 + item) * S
        return z_all[at:at + S]

    def y_merge(block, side, item, cz):
        tile = y_tiles[side][item // 4]
        start = (item % 4) * S
        target = 0 if side == 0 else 128 - S
        shift = (target + cz - start) % 128
        if shift:
            tile = pltpu.roll(tile, shift, 1)
        if side == 0:
            return jnp.concatenate([jnp.where(lane128 < S, tile, block[:, 0:128]), block[:, 128:]], axis=1)
        return jnp.concatenate([block[:, :CELLS - 128], jnp.where(lane128 >= 128 - S, tile, block[:, CELLS - 128:])], axis=1)

    def shift_x(block, side, item):
        row = x_rows[side * 8 + item:side * 8 + item + 1]
        if side == 0:
            return jnp.concatenate([row, block[:S - 1]], axis=0)
        return jnp.concatenate([block[1:], row], axis=0)

    for d, (cx, cy, cz) in enumerate(VELOCITY):
        block = pop[d].astype(F32)
        if cx:
            side = 0 if cx == 1 else 1
            block = shift_x(block, side, LEAVES[0][1 - side].index(d))
        shift = (S * cy + cz) % CELLS
        if shift:
            block = pltpu.roll(block, shift, 1)
        if cy:
            side = 0 if cy == 1 else 1
            block = y_merge(block, side, LEAVES[1][1 - side].index(d), cz)
        if cz:
            side = 0 if cz == 1 else 1
            edge = 0 if cz == 1 else S - 1
            block = jnp.where(depth == edge, z_ghost(side, LEAVES[2][1 - side].index(d)), block)
        pulled[d] = block
    here = sol[...]
    below, above = shift_x(here, 0, 5), shift_x(here, 1, 5)
    total = below + above
    grads[1] = above - below
    below = y_merge(pltpu.roll(here, S, 1), 0, 5, 0)
    above = y_merge(pltpu.roll(here, CELLS - S, 1), 1, 5, 0)
    total = total + below + above
    grads[2] = above - below
    below = jnp.where(depth == 0, z_ghost(0, 5), pltpu.roll(here, 1, 1))
    above = jnp.where(depth == S - 1, z_ghost(1, 5), pltpu.roll(here, CELLS - 1, 1))
    grads[3] = above - below
    grads[0] = total + below + above - 6.0 * here


def update(pulled, grads, sol, solid, rows, lanes, put):
    f = [pulled[d, rows, lanes] for d in range(19)]
    pair_sum = [f[i] + f[i + 1] for i in range(1, 19, 2)]
    pair_dif = [f[i] - f[i + 1] for i in range(1, 19, 2)]
    straight = pair_sum[0] + pair_sum[1] + pair_sum[2]
    slanted = (pair_sum[3] + pair_sum[4]) + (pair_sum[5] + pair_sum[6]) + (pair_sum[7] + pair_sum[8])
    density = f[0] * (1.0 / 3.0) + straight * (1.0 / 18.0) + slanted * (1.0 / 36.0)
    dif = pair_dif
    over = 1.0 / density
    over36 = over * (1.0 / 36.0)
    ux = (2.0 * dif[0] + ((dif[3] + dif[4]) + (dif[5] + dif[6]))) * over36
    uy = (2.0 * dif[1] + ((dif[3] - dif[4]) + (dif[7] + dif[8]))) * over36
    uz = (2.0 * dif[2] + ((dif[5] - dif[6]) + (dif[7] - dif[8]))) * over36
    amount = solid[rows, lanes]
    keep = 1.0 - amount
    if put is not None:
        scale = (1.0 / relax_time) * keep * density
        base = scale - (1.5 * scale) * (ux * ux + uy * uy + uz * uz)
        curve, slope = 4.5 * scale, 3.0 * scale
        rest = (1.0 / relax_time - 1.0) * keep
        even_part, odd_part = 0.5 * (amount - rest), 0.5 * (amount + rest)
        put(0, base + (amount - rest) * f[0])
        along_all = (ux, uy, uz, ux + uy, ux - uy, ux + uz, ux - uz, uy + uz, uy - uz)
        for pair in range(9):
            along = along_all[pair]
            even = base + (curve * along) * along + even_part * pair_sum[pair]
            odd = slope * along - odd_part * pair_dif[pair]
            put(2 * pair + 1, even + odd)
            put(2 * pair + 2, even - odd)
    mixed = (sol[rows, lanes] + diffusivity * grads[0, rows, lanes]
             - 0.5 * (ux * grads[1, rows, lanes] + uy * grads[2, rows, lanes] + uz * grads[3, rows, lanes]))
    reaction = rate_const * amount * keep * (saturation - mixed)
    return mixed + reaction, amount - reaction


def make_spread(spread):
    deep, lane = iota((128, CELLS), 0), iota((128, CELLS), 1)
    spread[...] = jnp.where(deep % S == lane // S, 1.0, 0.0).astype(BF16)


def chunks(body):
    for row in range(0, S, 16):
        for lane in range(0, CELLS, 128):
            body(slice(row, row + 16), slice(lane, lane + 128))


def front_kernel(front, redeal, pop, sol, solid, gx, gy, gz, send1, send2, send3, ones_ref, spread, pulled, grads):
    step = pl.program_id(0)

    @pl.when(step == 0)
    def _():
        make_spread(spread)

    ones_ref[...] = jnp.ones(ones_ref.shape, BF16)
    pull_block(pop.at[0], sol.at[0], gx.at[0], gy.at[0], gz.at[0], spread, pulled, grads)
    for target, ref in enumerate((send1, send2, send3)):
        @pl.when(step == target)
        def _():
            def one(rows, lanes):
                ref[0, rows, lanes], ref[1, rows, lanes] = update(pulled, grads, sol.at[0], solid.at[0], rows, lanes, None)

            chunks(one)


def rest_kernel(front, pop, sol, solid, gx, gy, gz, old_ref, new_pop, new_sol, new_solid, spread, pulled, grads):
    @pl.when(pl.program_id(0) == 0)
    def _():
        make_spread(spread)

    pull_block(pop.at[0], sol.at[0], gx.at[0], gy.at[0], gz.at[0], spread, pulled, grads)

    def one(rows, lanes):
        def put(direction, value):
            new_pop[0, direction, rows, lanes] = value.astype(BF16)

        new_sol[0, rows, lanes], new_solid[0, rows, lanes] = update(
            pulled, grads, sol.at[0], solid.at[0], rows, lanes, put)

    chunks(one)


def front_slot(step, front, redeal):
    group = front[0] // SLOTS % GROUPS
    slot = front[0] % SLOTS
    for entry in range(1, 3):
        ahead = (redeal[entry] // SLOTS % GROUPS - group + GROUPS) % GROUPS
        slot = jnp.where(ahead == step + 1, front[entry] % SLOTS, slot)
    return slot


def rest_slot(step, front):
    a, b, c = (front[entry] % SLOTS for entry in range(3))
    low, high = jnp.minimum(a, b), jnp.maximum(a, b)
    mid, high = jnp.minimum(high, c), jnp.maximum(high, c)
    low, mid = jnp.minimum(low, mid), jnp.maximum(low, mid)
    slot = step
    for taken in (low, mid, high):
        slot = slot + jnp.where(slot >= taken, 1, 0)
    return slot


def block_specs(pick):
    shapes = ((1, 19, S, CELLS), (1, S, CELLS), (1, S, CELLS), (1, 16, CELLS), (1, 2, S, 256), (1, 2, S, 256))
    return [pl.BlockSpec(shape, lambda step, *refs, n=len(shape): (pick(step, *refs),) + (0,) * (n - 1)) for shape in shapes]


WORK = [
    pltpu.VMEM((128, CELLS), BF16),
    pltpu.VMEM((19, S, CELLS), F32),
    pltpu.VMEM((4, S, CELLS), F32),
]


def front_update(front, redeal, populations, solute, solid_fraction, gx, gy, gz):
    specs = block_specs(front_slot)
    sent = pl.BlockSpec((2, S, CELLS), lambda *_: (0, 0, 0))
    return pl.pallas_call(
        front_kernel,
        out_shape=tuple(jax.ShapeDtypeStruct((2, S, CELLS), F32) for _ in range(3))
        + (jax.ShapeDtypeStruct(populations.shape, BF16),),
        grid_spec=pltpu.PrefetchScalarGridSpec(
            num_scalar_prefetch=2, grid=(3,), in_specs=specs, out_specs=(sent, sent, sent, specs[0]),
            scratch_shapes=WORK),
        compiler_params=pltpu.CompilerParams(vmem_limit_bytes=20 * 2**20),
        cost_estimate=pl.CostEstimate(flops=2 * 10**7, bytes_accessed=9 * 10**6, transcendentals=0),
        name="front",
    )(front, redeal, populations, solute, solid_fraction, gx, gy, gz)


def rest_update(front, populations, solute, solid_fraction, gx, gy, gz, new_populations):
    specs = block_specs(rest_slot)
    return pl.pallas_call(
        rest_kernel,
        out_shape=(
            jax.ShapeDtypeStruct(populations.shape, BF16),
            jax.ShapeDtypeStruct(solute.shape, F32),
            jax.ShapeDtypeStruct(solute.shape, F32),
        ),
        grid_spec=pltpu.PrefetchScalarGridSpec(
            num_scalar_prefetch=1, grid=(5,), in_specs=specs + [pl.BlockSpec(memory_space=pl.ANY)],
            out_specs=tuple(specs[:3]), scratch_shapes=WORK),
        input_output_aliases={7: 0},
        compiler_params=pltpu.CompilerParams(vmem_limit_bytes=20 * 2**20),
        cost_estimate=pl.CostEstimate(flops=10**8, bytes_accessed=16 * 10**6, transcendentals=0),
        name="rest",
    )(front, populations, solute, solid_fraction, gx, gy, gz, new_populations)


def place_kernel(front, table, got1, got2, got3, old_sol, old_solid, new_sol, new_solid, sems):
    group = front[0] // SLOTS % GROUPS
    copies = []
    for k, got in enumerate((got1, got2, got3)):
        source = (group + GROUPS - 1 - k) % GROUPS
        slot = table[source, 0, 0] % SLOTS
        for entry in range(1, 3):
            place = table[source, 0, entry]
            slot = jnp.where(place // SLOTS % GROUPS == group, place % SLOTS, slot)
        copies.append(pltpu.make_async_copy(got.at[0], new_sol.at[slot], sems.at[k, 0]))
        copies.append(pltpu.make_async_copy(got.at[1], new_solid.at[slot], sems.at[k, 1]))
    for copy in copies:
        copy.start()
    for copy in copies:
        copy.wait()


def place_front(front, table, received, new_solute, new_solid):
    smem, vmem, anywhere = (pl.BlockSpec(memory_space=m) for m in (pltpu.SMEM, pltpu.VMEM, pl.ANY))
    return pl.pallas_call(
        place_kernel,
        out_shape=tuple(jax.ShapeDtypeStruct(new_solute.shape, F32) for _ in range(2)),
        in_specs=[smem, smem] + [vmem] * 3 + [anywhere] * 2,
        out_specs=(anywhere, anywhere),
        input_output_aliases={5: 0, 6: 1},
        scratch_shapes=[pltpu.SemaphoreType.DMA((3, 2))],
        compiler_params=pltpu.CompilerParams(vmem_limit_bytes=2 * 2**20),
        cost_estimate=pl.CostEstimate(flops=0, bytes_accessed=2 * 10**6, transcendentals=0),
        name="place",
    )(front, table, *received, new_solute, new_solid)


def body(populations, solute, solid_fraction, neighbours, front_list, redeal_list):
    gx, gy, gz, table = exchange(populations, solute, neighbours, redeal_list)
    *sent, new_populations = front_update(front_list, redeal_list, populations, solute, solid_fraction, gx, gy, gz)
    received = [
        lax.ppermute(sent[k], "grp", [(g, (g + k + 1) % GROUPS) for g in range(GROUPS)]) for k in range(GROUPS - 1)
    ]
    new_populations, new_solute, new_solid = rest_update(
        front_list, populations, solute, solid_fraction, gx, gy, gz, new_populations)
    new_solute, new_solid = place_front(front_list, table, received, new_solute, new_solid)
    return new_populations, new_solute, new_solid


def solution(mesh):
    deal = ("blk", "grp")
    return jax.shard_map(
        body,
        mesh=mesh,
        in_specs=(P(deal, None, None, None), P(deal, None, None), P(deal, None, None), P(deal, None), P(deal), P(deal)),
        out_specs=(P(deal, None, None, None), P(deal, None, None), P(deal, None, None)),
        check_vma=False,
    )
```

```python
import jax
import jax.numpy as jnp
from jax import lax
from jax.experimental import pallas as pl
from jax.experimental.pallas import tpu as pltpu
from jax.sharding import PartitionSpec as P

VELOCITY = (
    (0, 0, 0), (1, 0, 0), (-1, 0, 0), (0, 1, 0), (0, -1, 0), (0, 0, 1), (0, 0, -1),
    (1, 1, 0), (-1, -1, 0), (1, -1, 0), (-1, 1, 0), (1, 0, 1), (-1, 0, -1), (1, 0, -1),
    (-1, 0, 1), (0, 1, 1), (0, -1, -1), (0, 1, -1), (0, -1, 1),
)
LEAVES = (
    ((2, 8, 10, 12, 14), (1, 7, 9, 11, 13)),
    ((4, 8, 9, 16, 18), (3, 7, 10, 15, 17)),
    ((6, 12, 13, 16, 17), (5, 11, 14, 15, 18)),
)
FETCH = (2, 8, 10, 12, 14, 1, 7, 9, 11, 13, 15, 16, 17, 18, 3, 4, 6, 5, 0)
SLOTS = 8
S = 32
CELLS = S * S
PEERS = 32
GROUPS = 4
TURNS = ((0, 1), (0, -1), (1, 0), (-1, 0), (1, 1), (-1, -1), (1, -1), (-1, 1))
WIDE = 256
F32, BF16, I32 = jnp.float32, jnp.bfloat16, jnp.int32
relax_time = 0.8
diffusivity = 0.1
rate_const = 0.5
saturation = 1.0


def iota(shape, dim):
    return lax.broadcasted_iota(I32, shape, dim)


def lane_shift(direction):
    return (S * VELOCITY[direction][1] + VELOCITY[direction][2]) % CELLS


def dot(a, b):
    return jnp.dot(a, b, preferred_element_type=F32)


def react(mixed, amount):
    reaction = rate_const * amount * (1.0 - amount) * (saturation - mixed)
    return mixed + reaction, amount - reaction


def front_slot(step, front, redeal):
    group = front[0] // SLOTS % GROUPS
    slot = front[0] % SLOTS
    for entry in range(1, 3):
        ahead = (redeal[entry] // SLOTS % GROUPS - group + GROUPS) % GROUPS
        slot = jnp.where(ahead == step + 1, front[entry] % SLOTS, slot)
    return slot


def rest_slot(step, front):
    a, b, c = (front[entry] % SLOTS for entry in range(3))
    low, high = jnp.minimum(a, b), jnp.maximum(a, b)
    mid, high = jnp.minimum(high, c), jnp.maximum(high, c)
    low, mid = jnp.minimum(low, mid), jnp.maximum(low, mid)
    slot = step
    for taken in (low, mid, high):
        slot = slot + jnp.where(slot >= taken, 1, 0)
    return slot


def place_slot(step, front, table):
    group = front[0] // SLOTS % GROUPS
    slot = table[step, 0, 0] % SLOTS
    for entry in range(1, 3):
        place = table[step, 0, entry]
        slot = jnp.where(place // SLOTS % GROUPS == group, place % SLOTS, slot)
    return slot


def exchange_kernel(pop_hbm, sol_hbm, solid_hbm, nbr_hbm, front_hbm, redeal_hbm,
                    moved, flow, fresh, got_mixed, got_solid, table_ref,
                    sol_ref, solid_ref, xr, fx, fy, fz, lx, ly, ey, ez, s1, s2, s3, r1, r2, r3, mine, inv_vmem,
                    keep, spread, ghost, grads, out_mixed, out_solid,
                    nbr, inv, front, redeal, fetch_sem, small_sem, send_sem, recv_sem, grp_send, grp_recv):
    me = lax.axis_index("blk")
    grp = lax.axis_index("grp")

    def fetch(direction):
        return pltpu.make_async_copy(pop_hbm.at[:, direction], moved.at[:, direction], fetch_sem.at[direction])

    nbr_copy = pltpu.make_async_copy(nbr_hbm, nbr, small_sem.at[0])
    redeal_copy = pltpu.make_async_copy(redeal_hbm, redeal, small_sem.at[1])
    inv_copy = pltpu.make_async_copy(inv_vmem, inv, small_sem.at[2])
    sol_copy = pltpu.make_async_copy(sol_hbm, sol_ref, small_sem.at[3])
    front_copy = pltpu.make_async_copy(front_hbm, front, small_sem.at[4])
    solid_copy = pltpu.make_async_copy(solid_hbm, solid_ref, small_sem.at[5])
    nbr_copy.start()
    redeal_copy.start()
    front_copy.start()
    sol_copy.start()
    for direction in FETCH:
        fetch(direction).start()

    solid_copy.start()
    barrier = pltpu.get_barrier_semaphore()

    @pl.loop(1, PEERS)
    def _(k):
        pl.semaphore_signal(barrier, inc=1, device_id={"blk": (me + k) % PEERS}, device_id_type=pl.DeviceIdType.MESH)

    for k in range(1, GROUPS):
        pl.semaphore_signal(barrier, inc=1, device_id={"grp": (grp + k) % GROUPS}, device_id_type=pl.DeviceIdType.MESH)

    deep, lane = iota((CELLS, 128), 0), iota((CELLS, 128), 1) % S
    pick = [jnp.where(deep == lane * S + z, 1.0, 0.0).astype(BF16) for z in (0, S - 1)]
    wide, lane = iota((128, 128), 0), iota((128, 128), 1) % S
    pick_y = [jnp.where(wide == lane + first, 1.0, 0.0).astype(BF16) for first in (0, 128 - S)]

    nbr_copy.wait()
    redeal_copy.wait()
    front_copy.wait()

    def owner(slot, face):
        return nbr[slot, face] // (SLOTS * GROUPS)

    row8, lane8 = iota((8, 128), 0), iota((8, 128), 1)
    found = jnp.zeros((8, 128), I32)
    for axis in range(3):
        hit = jnp.zeros((8, 128), I32)
        for slot in range(SLOTS):
            for side in range(2):
                hit = jnp.where(lane8 == owner(slot, 2 * axis + side), 2 * slot + side, hit)
        found = jnp.where(row8 == axis, hit, found)
    inv_vmem[...] = found
    inv_copy.start()
    lane1 = iota((1, 128), 1)
    mine[...] = jnp.where(lane1 == 0, redeal[0], jnp.where(lane1 == 1, redeal[1], redeal[2]))
    sol_copy.wait()

    fetched = set()

    def ready(directions):
        for direction in directions:
            if direction not in fetched:
                fetched.add(direction)
                fetch(direction).wait()

    ready(LEAVES[0][0] + LEAVES[0][1])

    @pl.loop(0, SLOTS)
    def _(slot):
        faces = []
        for side in range(2):
            at, row = (16, 15) if side else (0, 0)
            rows = [moved[slot, d, at:at + 16, :].astype(F32)[row:row + 1] for d in LEAVES[0][side]]
            rows.append(sol_ref[slot, at + row:at + row + 1, :])
            rows.append(jnp.zeros((2, CELLS), F32))
            rows = jnp.concatenate(rows, axis=0)
            faces.append(rows)
        xr[slot] = jnp.concatenate(faces, axis=0).astype(BF16)

    faces = xr[...].reshape(SLOTS * 16, CELLS)
    z_low, z_top = dot(faces, pick[0]), dot(faces, pick[1])
    y_low, y_top = dot(faces[:, 0:128], pick_y[0]), dot(faces[:, CELLS - 128:], pick_y[1])
    quarter1 = lane1 // S
    ready((15, 16, 17, 18))
    high = slice(CELLS - 128, CELLS)
    lane16 = iota((16, 128), 1)

    def across(d, at, z):
        one = jnp.where(lane16 == z, 1.0, 0.0).astype(BF16)
        tile = moved[:, d, :, at].reshape(SLOTS * S, 128)
        return lax.dot_general(one, tile, (((1,), (1,)), ((), ())), preferred_element_type=F32)

    y_lines = ((across(16, slice(0, 128), 0), across(18, slice(0, 128), S - 1)),
               (across(15, high, 127), across(17, high, 128 - S)))
    for slot in range(SLOTS):
        for side in range(2):
            row = slot * 16 + side * 8
            four = (y_top, y_low, z_top, z_low) if side else (y_low, y_top, z_low, z_top)
            four = [part[row + 1 + i:row + 2 + i] for i, part in enumerate(four)]
            line = jnp.where(quarter1 == 0, four[0], jnp.where(quarter1 == 1, four[1], jnp.where(quarter1 == 2, four[2], four[3])))
            lx[2 * slot + side] = jnp.broadcast_to(line, (16, 128)).astype(BF16)
            tiles = [part[:, 128 * (slot // 4):128 * (slot // 4) + 128] for part in y_lines[side]]
            shift = (128 - S * (slot % 4)) % 128
            if shift:
                tiles[0] = pltpu.roll(tiles[0], shift, 1)
            shift = (shift + S) % 128
            if shift:
                tiles[1] = pltpu.roll(tiles[1], shift, 1)
            ly[2 * slot + side] = jnp.where(lane16 < S, tiles[0], tiles[1]).astype(BF16)

    inv_copy.wait()
    pl.semaphore_wait(barrier, PEERS - 1 + GROUPS - 1)

    def send(src, dst, which, peer):
        return pltpu.make_async_remote_copy(
            src_ref=src.at[peer], dst_ref=dst.at[me], send_sem=send_sem.at[which], recv_sem=recv_sem.at[which],
            device_id={"blk": peer}, device_id_type=pl.DeviceIdType.MESH)

    def all_of(src, dst, which):
        return pltpu.make_async_remote_copy(
            src_ref=src.at[pl.ds(0, PEERS - 1)], dst_ref=dst.at[pl.ds(0, PEERS - 1)], send_sem=send_sem.at[which],
            recv_sem=recv_sem.at[which], device_id={"blk": (me + 1) % PEERS}, device_id_type=pl.DeviceIdType.MESH)

    def grp_copy(src, dst, which, k):
        return pltpu.make_async_remote_copy(
            src_ref=src, dst_ref=dst, send_sem=grp_send.at[which, k], recv_sem=grp_recv.at[which, k],
            device_id={"grp": (grp + k) % GROUPS}, device_id_type=pl.DeviceIdType.MESH)

    def table_copy(k):
        return grp_copy(mine, table_ref.at[k - 1], 0, k)

    def solid_out(k):
        return grp_copy(out_solid.at[k - 1], got_solid.at[k - 1], 1, k)

    def mixed_out(k):
        return grp_copy(out_mixed.at[k - 1], got_mixed.at[k - 1], 2, k)

    upper8 = iota((16, 128), 0) < 8

    @pl.loop(1, PEERS)
    def _(k):
        peer = (me + k) % PEERS
        s1[peer] = jnp.where(upper8, lx[inv[0, peer]].astype(F32), ly[inv[1, peer]].astype(F32)).astype(BF16)
        send(s1, r1, 0, peer).start()

    for k in range(1, GROUPS):
        table_copy(k).start()

    quarter = iota((SLOTS * S, 128), 1) // S

    def place_items(into, side, parts, later):
        low = jnp.where(quarter == 0, parts[0], jnp.where(quarter == 1, parts[1], jnp.where(quarter == 2, parts[2], parts[3])))
        late = jnp.where(quarter == later, parts[4], parts[5])
        low, late = low.reshape(SLOTS, S, 128).astype(BF16), late.reshape(SLOTS, S, 128).astype(BF16)
        for slot in range(SLOTS):
            into[2 * slot + side, :, 0:128] = low[slot]
            into[2 * slot + side, :, 128:256] = late[slot]

    sol = sol_ref[...].reshape(SLOTS * S, CELLS).astype(BF16)
    for side in range(2):
        ready(LEAVES[1][side])
        at = high if side else slice(0, 128)
        parts = [dot(moved[:, d, :, at].reshape(SLOTS * S, 128), pick_y[side]) for d in LEAVES[1][side]]
        parts.append(dot(sol[:, at], pick_y[side]))
        place_items(fy, side, parts, 0)
    for side in range(2):
        ready(LEAVES[2][side])
        parts = [dot(moved[:, d].reshape(SLOTS * S, CELLS), pick[side]) for d in LEAVES[2][side]] + [dot(sol, pick[side])]
        place_items(fz, side, parts, 2)

    left = iota((S, 128), 1) < 64

    @pl.loop(1, PEERS)
    def _(k):
        peer = (me + k) % PEERS
        y_part, z_part = fy[inv[1, peer]], fz[inv[2, peer]]
        s2[peer, :, 0:128] = y_part[:, 0:128]
        s2[peer, :, 128:256] = jnp.where(left, y_part[:, 128:].astype(F32), z_part[:, 128:].astype(F32)).astype(BF16)
        s2[peer, :, 256:384] = z_part[:, 0:128]
        send(s2, r2, 1, peer).start()

    row8w, lane8w = iota((8, CELLS), 0), iota((8, CELLS), 1)
    for i, (cy, cz) in enumerate(TURNS):
        hold = lane8w >= 0
        if cy:
            hold = hold & ((lane8w >= S) if cy == 1 else (lane8w < CELLS - S))
        if cz:
            hold = hold & (lane8w % S != (0 if cz == 1 else S - 1))
        keep[i] = jnp.where(hold, 1.0, 0.0)

    @pl.loop(0, SLOTS)
    def _(slot):
        for side in range(2):
            rows = xr[slot, 8 * side:8 * side + 8, :].astype(F32)
            turned = rows
            for i, d in enumerate(LEAVES[0][side]):
                shift = lane_shift(d)
                if shift:
                    turned = jnp.where(row8w == i, pltpu.roll(rows, shift, 1) * keep[TURNS.index(VELOCITY[d][1:])], turned)
            fx[2 * slot + side] = jnp.concatenate([turned[:, :512], turned[:, 512:]], axis=0).astype(BF16)

    all_of(s1, r1, 0).wait_recv()

    def lines(face, row):
        return jnp.concatenate([r1[owner(slot, face)].astype(F32)[row:row + 1] for slot in range(SLOTS)], axis=0)

    x_lo, x_hi, y_lo, y_hi = lines(0, 0), lines(1, 0), lines(2, 8), lines(3, 8)
    quarter8 = lane8 // S
    back = [pltpu.roll(part, 128 - S, 1) for part in (x_lo, x_hi, y_lo, y_hi)]
    x_lo, x_hi = pltpu.roll(x_lo, S, 1), pltpu.roll(x_hi, S, 1)

    def four_of(one, two, three, zero):
        return jnp.where(quarter8 == 1, one, jnp.where(quarter8 == 2, two, jnp.where(quarter8 == 3, three, zero)))

    y_rows = (jnp.where(quarter8 == 1, x_hi, x_lo), jnp.where(quarter8 == 1, x_lo, x_hi))
    z_rows = (four_of(back[1], back[0], back[3], back[2]), four_of(back[0], back[1], back[2], back[3]))
    for slot in range(SLOTS):
        for side in range(2):
            ey[2 * slot + side] = jnp.broadcast_to(y_rows[side][slot:slot + 1], (16, 128))
            ez[2 * slot + side] = jnp.broadcast_to(z_rows[side][slot:slot + 1], (16, 128))
    row16 = iota((16, 128), 0)

    @pl.loop(1, PEERS)
    def _(k):
        peer = (me + k) % PEERS
        part = fx[inv[0, peer]]
        first = jnp.where(row16 == 6, ey[inv[1, peer]], jnp.where(row16 == 7, ez[inv[2, peer]], part[:, 0:128].astype(F32)))
        s3[peer, :, 0:128] = first.astype(BF16)
        s3[peer, :, 128:512] = part[:, 128:512]
        send(s3, r3, 2, peer).start()

    ready((0,))
    solid_copy.wait()
    for k in range(1, GROUPS):
        out_solid[k - 1] = solid_ref[front_slot(k - 1, front, redeal)]
        solid_out(k).start()
    deep, lane = iota((128, CELLS), 0), iota((128, CELLS), 1)
    for side in range(2):
        spread[side] = jnp.where((deep % S == lane // S) & (lane % S == (S - 1) * side), 1.0, 0.0).astype(BF16)
    row8w = iota((8, CELLS), 0)
    depth8w = lane8w % S

    def without_row(block, step):
        if step == 1:
            return jnp.concatenate([jnp.where(row8w == 0, 0.0, block[:8]), block[8:]], axis=0)
        return jnp.concatenate([block[:S - 8], jnp.where(row8w == 7, 0.0, block[S - 8:])], axis=0)

    def masked(block, turn):
        tall = keep[TURNS.index(turn)]
        return block * jnp.concatenate([tall] * 4, axis=0)

    @pl.loop(0, SLOTS)
    def _(slot):
        for d, (step, cy, cz) in enumerate(VELOCITY):
            shift = lane_shift(d)
            if d:
                block = moved[slot, d].astype(F32)
                if step:
                    block = without_row(pltpu.roll(block, step % S, 0), step)
                if shift:
                    block = masked(pltpu.roll(block, shift, 1), (cy, cz))
                moved[slot, d] = block.astype(BF16)
        here = sol_ref[slot]
        below, above = without_row(pltpu.roll(here, 1, 0), 1), without_row(pltpu.roll(here, S - 1, 0), -1)
        total = below + above
        grads[slot, 1] = above - below
        below, above = masked(pltpu.roll(here, S, 1), (1, 0)), masked(pltpu.roll(here, CELLS - S, 1), (-1, 0))
        total = total + below + above
        grads[slot, 2] = above - below
        below, above = masked(pltpu.roll(here, 1, 1), (0, 1)), masked(pltpu.roll(here, CELLS - 1, 1), (0, -1))
        grads[slot, 3] = above - below
        grads[slot, 0] = here + diffusivity * (total + below + above - 6.0 * here)

    all_of(s2, r2, 1).wait_recv()
    all_of(s3, r3, 2).wait_recv()
    row32, lane32 = iota((S, 128), 0), iota((S, 128), 1)
    item = lane32 // S
    depth32 = lane32 % S
    row16w = iota((16, CELLS), 0)

    def shift_rows(plane, down, up, edge):
        from_low = jnp.where(row32 == 0, edge, pltpu.roll(plane, 1, 0))
        from_high = jnp.where(row32 == S - 1, edge, pltpu.roll(plane, S - 1, 0))
        return jnp.where(item == down, from_low, jnp.where(item == up, from_high, plane))

    @pl.loop(0, SLOTS)
    def _(slot):
        for side in range(2):
            enter = LEAVES[0][1 - side]
            part = r3[owner(slot, side)].astype(F32)
            rows = jnp.concatenate([part[0:8], part[8:16]], axis=1)
            at, hit = (0, row16w == 0) if side == 0 else (16, row16w == 15)
            for i, d in enumerate(enter):
                moved[slot, d, at:at + 16, :] += jnp.where(hit, rows[i:i + 1], 0.0).astype(BF16)
            at, hit, sign = (0, row8w == 0, -1.0) if side == 0 else (S - 8, row8w == 7, 1.0)
            extra = jnp.where(hit, rows[5:6], 0.0)
            grads[slot, 0, at:at + 8, :] += diffusivity * extra
            grads[slot, 1, at:at + 8, :] += sign * extra

            enter = LEAVES[1][1 - side]
            down, up = (1, 2) if side == 0 else (2, 1)
            peer = owner(slot, 2 + side)
            edge = r3[peer, :, 0:128].astype(F32)[6:7]
            tiles = (shift_rows(r2[peer, :, 0:128].astype(F32), down, up, edge), r2[peer, :, 128:256].astype(F32))
            first = 0 if side == 0 else 128 - S
            at = 0 if side == 0 else CELLS - 128
            for i in range(6):
                cz = VELOCITY[enter[i]][2] if i < 5 else 0
                shift = (first + cz - (i % 4) * S) % 128
                tile = tiles[i // 4]
                if shift:
                    tile = pltpu.roll(tile, shift, 1)
                hit = item == first // S
                if cz:
                    hit = hit & (depth32 != (0 if cz == 1 else S - 1))
                tile = jnp.where(hit, tile, 0.0)
                if i < 5:
                    moved[slot, enter[i], :, at:at + 128] += tile.astype(BF16)
                else:
                    grads[slot, 0, :, at:at + 128] += diffusivity * tile
                    grads[slot, 2, :, at:at + 128] += sign * tile

            enter = LEAVES[2][1 - side]
            peer = owner(slot, 4 + side)
            edge = r3[peer, :, 0:128].astype(F32)[7:8]
            third = jnp.sum(jnp.where(lane32 == row32 + 96, edge, 0.0), axis=1, keepdims=True)
            fourth = jnp.sum(jnp.where(lane32 == row32, edge, 0.0), axis=1, keepdims=True)
            plane, late = r2[peer, :, 256:384].astype(F32), r2[peer, :, 128:256].astype(F32)
            turn, at3, at4 = (1, 96, 95) if side == 0 else (127, 127, 64)
            turned = jnp.where(lane32 == at3, third, pltpu.roll(plane, turn, 1))
            turned_late = jnp.where(lane32 == at4, fourth, pltpu.roll(late, 128 - turn, 1))
            plane = jnp.where(item == 3, turned, shift_rows(plane, down, up, edge))
            late = jnp.where(item == 2, turned_late, late)
            stack = [jnp.where(item == i, plane, 0.0).astype(BF16) for i in range(4)]
            stack += [jnp.where(item == i, late, 0.0).astype(BF16) for i in range(2, 4)]
            ghost[...] = dot(jnp.concatenate(stack, axis=0), spread[side])
            for i, d in enumerate(enter):
                moved[slot, d] += ghost[S * i:S * i + S, :].astype(BF16)
            grads[slot, 0] += diffusivity * ghost[5 * S:6 * S, :]
            grads[slot, 3] += sign * ghost[5 * S:6 * S, :]

    def moments(slot, lanes):
        def f(d):
            return moved[slot, d, :, lanes].astype(F32)

        straight, slanted = 0.0, 0.0
        along = [0.0, 0.0, 0.0]
        for d in range(1, 19, 2):
            one, two = f(d), f(d + 1)
            both, diff = one + two, one - two
            if d < 7:
                straight = both + straight
                along[d // 2] = diff + diff
            else:
                slanted = both + slanted
                for axis in range(3):
                    if VELOCITY[d][axis]:
                        along[axis] = along[axis] + diff if VELOCITY[d][axis] == 1 else along[axis] - diff
        density = f(0) * (1.0 / 3.0) + straight * (1.0 / 18.0) + slanted * (1.0 / 36.0)
        over36 = (1.0 / 36.0) / density
        ux, uy, uz = (part * over36 for part in along)
        mixed = grads[slot, 0, :, lanes] - 0.5 * (
            ux * grads[slot, 1, :, lanes] + uy * grads[slot, 2, :, lanes] + uz * grads[slot, 3, :, lanes])
        return density, ux, uy, uz, mixed

    @pl.loop(0, GROUPS - 1)
    def _(step):
        slot = front_slot(step, front, redeal)

        @pl.loop(0, CELLS // WIDE)
        def _(part):
            lanes = pl.ds(pl.multiple_of(part * WIDE, WIDE), WIDE)
            out_mixed[step, :, lanes] = moments(slot, lanes)[4]

        mixed_out(step + 1).start()

    @pl.loop(0, SLOTS - 3)
    def _(step):
        slot = rest_slot(step, front)

        @pl.loop(0, CELLS // WIDE)
        def _(part):
            lanes = pl.ds(pl.multiple_of(part * WIDE, WIDE), WIDE)
            *now, mixed = moments(slot, lanes)
            for i in range(4):
                flow[step, i, :, lanes] = now[i]
            fresh[step, 0, :, lanes], fresh[step, 1, :, lanes] = react(mixed, solid_ref[slot, :, lanes])

    all_of(s1, r1, 0).wait_send()
    all_of(s2, r2, 1).wait_send()
    all_of(s3, r3, 2).wait_send()
    for k in range(1, GROUPS):
        table_copy(k).wait()
        solid_out(k).wait()
        mixed_out(k).wait()


def exchange(populations, solute, solid_fraction, neighbours, front_list, redeal_list):
    vmem, hbm = (pl.BlockSpec(memory_space=m) for m in (pltpu.VMEM, pltpu.HBM))
    operands = (populations, solute, solid_fraction, neighbours, front_list, redeal_list)
    return pl.pallas_call(
        exchange_kernel,
        out_shape=(
            jax.ShapeDtypeStruct(populations.shape, BF16),
            jax.ShapeDtypeStruct((SLOTS - 3, 4, S, CELLS), F32),
            jax.ShapeDtypeStruct((SLOTS - 3, 2, S, CELLS), F32),
            jax.ShapeDtypeStruct((GROUPS - 1, S, CELLS), F32),
            jax.ShapeDtypeStruct((GROUPS - 1, S, CELLS), F32),
            jax.ShapeDtypeStruct((GROUPS - 1, 1, 128), I32),
        ),
        in_specs=[hbm] * 6,
        out_specs=(vmem,) * 6,
        scratch_shapes=[
            pltpu.VMEM((SLOTS, S, CELLS), F32),
            pltpu.VMEM((SLOTS, S, CELLS), F32),
            pltpu.VMEM((SLOTS, 16, CELLS), BF16),
            pltpu.VMEM((2 * SLOTS, 16, 512), BF16),
            pltpu.VMEM((2 * SLOTS, S, 256), BF16),
            pltpu.VMEM((2 * SLOTS, S, 256), BF16),
            pltpu.VMEM((2 * SLOTS, 16, 128), BF16),
            pltpu.VMEM((2 * SLOTS, 16, 128), BF16),
            pltpu.VMEM((2 * SLOTS, 16, 128), F32),
            pltpu.VMEM((2 * SLOTS, 16, 128), F32),
            pltpu.VMEM((PEERS, 16, 128), BF16),
            pltpu.VMEM((PEERS, S, 384), BF16),
            pltpu.VMEM((PEERS, 16, 512), BF16),
            pltpu.VMEM((PEERS, 16, 128), BF16),
            pltpu.VMEM((PEERS, S, 384), BF16),
            pltpu.VMEM((PEERS, 16, 512), BF16),
            pltpu.VMEM((1, 128), I32),
            pltpu.VMEM((8, 128), I32),
            pltpu.VMEM((len(TURNS), 8, CELLS), F32),
            pltpu.VMEM((2, 128, CELLS), BF16),
            pltpu.VMEM((6 * S, CELLS), F32),
            pltpu.VMEM((SLOTS, 4, S, CELLS), F32),
            pltpu.VMEM((GROUPS - 1, S, CELLS), F32),
            pltpu.VMEM((GROUPS - 1, S, CELLS), F32),
            pltpu.SMEM((SLOTS, 6), I32),
            pltpu.SMEM((8, 128), I32),
            pltpu.SMEM((3,), I32),
            pltpu.SMEM((3,), I32),
            pltpu.SemaphoreType.DMA((19,)),
            pltpu.SemaphoreType.DMA((6,)),
            pltpu.SemaphoreType.DMA((3,)),
            pltpu.SemaphoreType.DMA((3,)),
            pltpu.SemaphoreType.DMA((3, GROUPS)),
            pltpu.SemaphoreType.DMA((3, GROUPS)),
        ],
        compiler_params=pltpu.CompilerParams(collective_id=0, has_side_effects=True, vmem_limit_bytes=28 * 2**20),
        cost_estimate=pl.CostEstimate(flops=10**9, bytes_accessed=12 * 10**6, transcendentals=0),
        name="exchange",
    )(*(pltpu.with_memory_space_constraint(operand, pltpu.HBM) for operand in operands))


def collide(f, flow, amount, put):
    density, ux, uy, uz = flow
    pair_sum = [f[i] + f[i + 1] for i in range(1, 19, 2)]
    pair_dif = [f[i] - f[i + 1] for i in range(1, 19, 2)]
    share = 1.0 - amount
    scale = (1.0 / relax_time) * share * density
    base = scale - (1.5 * scale) * (ux * ux + uy * uy + uz * uz)
    curve, slope = 4.5 * scale, 3.0 * scale
    rest = (1.0 / relax_time - 1.0) * share
    even_part, odd_part = 0.5 * (amount - rest), 0.5 * (amount + rest)
    put(0, base + (amount - rest) * f[0])
    along_all = (ux, uy, uz, ux + uy, ux - uy, ux + uz, ux - uz, uy + uz, uy - uz)
    for pair in range(9):
        along = along_all[pair]
        even = base + (curve * along) * along + even_part * pair_sum[pair]
        odd = slope * along - odd_part * pair_dif[pair]
        put(2 * pair + 1, even + odd)
        put(2 * pair + 2, even - odd)


def collide_kernel(front, table, moved, flow, fresh, got_mixed, got_solid, solid, new_pop, new_sol, new_solid,
                   ones, done, placed, sems, pop_sems):
    ones[...] = jnp.ones(ones.shape, BF16)
    copies = []
    for k in range(3):
        slot = place_slot(k, front, table)
        placed[0, k], placed[1, k] = react(got_mixed[k], got_solid[k])
        copies.append(pltpu.make_async_copy(ones, new_pop.at[slot], sems.at[0, k]))
        copies.append(pltpu.make_async_copy(placed.at[0, k], new_sol.at[slot], sems.at[1, k]))
        copies.append(pltpu.make_async_copy(placed.at[1, k], new_solid.at[slot], sems.at[2, k]))
    for k in range(SLOTS - 3):
        slot = rest_slot(k, front)
        copies.append(pltpu.make_async_copy(fresh.at[k, 0], new_sol.at[slot], sems.at[1, 3 + k]))
        copies.append(pltpu.make_async_copy(fresh.at[k, 1], new_solid.at[slot], sems.at[2, 3 + k]))
    for copy in copies:
        copy.start()

    def out(index):
        return pltpu.make_async_copy(done.at[index], new_pop.at[rest_slot(index, front)], pop_sems.at[index])

    @pl.loop(0, SLOTS - 3)
    def _(index):
        slot = rest_slot(index, front)
        for row in range(0, S, 16):
            for lane in range(0, CELLS, 128):
                rows, lanes = slice(row, row + 16), slice(lane, lane + 128)

                def put(direction, value):
                    done[index, direction, rows, lanes] = value.astype(BF16)

                f = [moved[slot, d, rows, lanes].astype(F32) for d in range(19)]
                collide(f, [flow[index, i, rows, lanes] for i in range(4)], solid[slot, rows, lanes], put)
        out(index).start()

    for copy in copies:
        copy.wait()
    for index in range(SLOTS - 3):
        out(index).wait()


def collide_all(front, table, moved, flow, fresh, got_mixed, got_solid, solid_fraction):
    smem, vmem, anywhere = (pl.BlockSpec(memory_space=m) for m in (pltpu.SMEM, pltpu.VMEM, pl.ANY))
    return pl.pallas_call(
        collide_kernel,
        out_shape=(
            jax.ShapeDtypeStruct(moved.shape, BF16),
            jax.ShapeDtypeStruct(solid_fraction.shape, F32),
            jax.ShapeDtypeStruct(solid_fraction.shape, F32),
        ),
        in_specs=[smem] * 2 + [vmem] * 6,
        out_specs=(anywhere,) * 3,
        scratch_shapes=[
            pltpu.VMEM((19, S, CELLS), BF16),
            pltpu.VMEM((SLOTS - 3, 19, S, CELLS), BF16),
            pltpu.VMEM((2, 3, S, CELLS), F32),
            pltpu.SemaphoreType.DMA((3, SLOTS)),
            pltpu.SemaphoreType.DMA((SLOTS - 3,)),
        ],
        compiler_params=pltpu.CompilerParams(vmem_limit_bytes=16 * 2**20),
        cost_estimate=pl.CostEstimate(flops=10**8, bytes_accessed=16 * 10**6, transcendentals=0),
        name="collide",
    )(front, table, moved, flow, fresh, got_mixed, got_solid, solid_fraction)


def body(populations, solute, solid_fraction, neighbours, front_list, redeal_list):
    moved, flow, fresh, got_mixed, got_solid, table = exchange(
        populations, solute, solid_fraction, neighbours, front_list, redeal_list)
    return collide_all(front_list, table, moved, flow, fresh, got_mixed, got_solid, solid_fraction)


def solution(mesh):
    deal = ("blk", "grp")
    return jax.shard_map(
        body,
        mesh=mesh,
        in_specs=(P(deal, None, None, None), P(deal, None, None), P(deal, None, None), P(deal, None), P(deal), P(deal)),
        out_specs=(P(deal, None, None, None), P(deal, None, None), P(deal, None, None)),
        check_vma=False,
    )
```

```python
import jax
import jax.numpy as jnp
from jax import lax
from jax.experimental import pallas as pl
from jax.experimental.pallas import tpu as pltpu
from jax.sharding import PartitionSpec as P

VELOCITY = (
    (0, 0, 0), (1, 0, 0), (-1, 0, 0), (0, 1, 0), (0, -1, 0), (0, 0, 1), (0, 0, -1),
    (1, 1, 0), (-1, -1, 0), (1, -1, 0), (-1, 1, 0), (1, 0, 1), (-1, 0, -1), (1, 0, -1),
    (-1, 0, 1), (0, 1, 1), (0, -1, -1), (0, 1, -1), (0, -1, 1),
)
LEAVES = (
    ((2, 8, 10, 12, 14), (1, 7, 9, 11, 13)),
    ((4, 8, 9, 16, 18), (3, 7, 10, 15, 17)),
    ((6, 12, 13, 16, 17), (5, 11, 14, 15, 18)),
)
FETCH = (2, 8, 10, 12, 14, 1, 7, 9, 11, 13, 15, 16, 17, 18, 3, 4, 6, 5, 0)
SLOTS = 8
S = 32
CELLS = S * S
PEERS = 32
GROUPS = 4
TURNS = ((0, 1), (0, -1), (1, 0), (-1, 0), (1, 1), (-1, -1), (1, -1), (-1, 1))
WIDE = 256
F32, BF16, I32 = jnp.float32, jnp.bfloat16, jnp.int32
relax_time = 0.8
diffusivity = 0.1
rate_const = 0.5
saturation = 1.0


def iota(shape, dim):
    return lax.broadcasted_iota(I32, shape, dim)


def lane_shift(direction):
    return (S * VELOCITY[direction][1] + VELOCITY[direction][2]) % CELLS


def dot(a, b):
    return jnp.dot(a, b, preferred_element_type=F32)


def react(mixed, amount):
    reaction = rate_const * amount * (1.0 - amount) * (saturation - mixed)
    return mixed + reaction, amount - reaction


def front_slot(step, front, redeal):
    group = (front[0] >> 3) & (GROUPS - 1)
    slot = front[0] & (SLOTS - 1)
    for entry in range(1, 3):
        ahead = ((redeal[entry] >> 3) - group) & (GROUPS - 1)
        slot = jnp.where(ahead == step + 1, front[entry] & (SLOTS - 1), slot)
    return slot


def rest_slot(step, front):
    a, b, c = (front[entry] & (SLOTS - 1) for entry in range(3))
    low, high = jnp.minimum(a, b), jnp.maximum(a, b)
    mid, high = jnp.minimum(high, c), jnp.maximum(high, c)
    low, mid = jnp.minimum(low, mid), jnp.maximum(low, mid)
    slot = step
    for taken in (low, mid, high):
        slot = slot + jnp.where(slot >= taken, 1, 0)
    return slot


def place_slot(step, front, table):
    group = (front[0] >> 3) & (GROUPS - 1)
    slot = table[step, 0, 0] & (SLOTS - 1)
    for entry in range(1, 3):
        place = table[step, 0, entry]
        slot = jnp.where((place >> 3) & (GROUPS - 1) == group, place & (SLOTS - 1), slot)
    return slot


def exchange_kernel(pop_hbm, sol_hbm, solid_hbm, nbr_hbm, front_hbm, redeal_hbm,
                    moved, flow, fresh, got_mixed, got_base, got_solid, table_ref,
                    sol_ref, solid_ref, xr, fx, fy, fz, lx, ly, ey, ez, s1, s2, s3, r1, r2, r3, mine, inv_vmem,
                    keep, spread, ghost, grads, edge_in, edge_rows, out_mixed, out_base, out_solid,
                    nbr, inv, front, redeal, fetch_sem, small_sem, send_sem, recv_sem, grp_send, grp_recv):
    me = lax.axis_index("blk")
    grp = lax.axis_index("grp")

    def fetch(direction):
        return pltpu.make_async_copy(pop_hbm.at[:, direction], moved.at[:, direction], fetch_sem.at[direction])

    nbr_copy = pltpu.make_async_copy(nbr_hbm, nbr, small_sem.at[0])
    redeal_copy = pltpu.make_async_copy(redeal_hbm, redeal, small_sem.at[1])
    inv_copy = pltpu.make_async_copy(inv_vmem, inv, small_sem.at[2])
    sol_copy = pltpu.make_async_copy(sol_hbm, sol_ref, small_sem.at[3])
    front_copy = pltpu.make_async_copy(front_hbm, front, small_sem.at[4])
    solid_copy = pltpu.make_async_copy(solid_hbm, solid_ref, small_sem.at[5])
    nbr_copy.start()
    redeal_copy.start()
    front_copy.start()
    sol_copy.start()
    for direction in FETCH:
        fetch(direction).start()

    solid_copy.start()
    barrier = pltpu.get_barrier_semaphore()

    @pl.loop(1, PEERS)
    def _(k):
        pl.semaphore_signal(barrier, inc=1, device_id={"blk": (me + k) % PEERS}, device_id_type=pl.DeviceIdType.MESH)

    for k in range(1, GROUPS):
        pl.semaphore_signal(barrier, inc=1, device_id={"grp": (grp + k) % GROUPS}, device_id_type=pl.DeviceIdType.MESH)

    deep, lane = iota((CELLS, 128), 0), iota((CELLS, 128), 1) & (S - 1)
    pick = [jnp.where(deep == lane * S + z, 1.0, 0.0).astype(BF16) for z in (0, S - 1)]
    wide, lane = iota((128, 128), 0), iota((128, 128), 1) & (S - 1)
    pick_y = [jnp.where(wide == lane + first, 1.0, 0.0).astype(BF16) for first in (0, 128 - S)]

    nbr_copy.wait()
    redeal_copy.wait()
    front_copy.wait()

    def owner(slot, face):
        return nbr[slot, face] >> 5

    row8, lane8 = iota((8, 128), 0), iota((8, 128), 1)
    found = jnp.zeros((8, 128), I32)
    for axis in range(3):
        hit = jnp.zeros((8, 128), I32)
        for slot in range(SLOTS):
            for side in range(2):
                hit = jnp.where(lane8 == owner(slot, 2 * axis + side), 2 * slot + side, hit)
        found = jnp.where(row8 == axis, hit, found)
    inv_vmem[...] = found
    inv_copy.start()
    lane1 = iota((1, 128), 1)
    mine[...] = jnp.where(lane1 == 0, redeal[0], jnp.where(lane1 == 1, redeal[1], redeal[2]))
    sol_copy.wait()

    fetched = set()

    def ready(directions):
        for direction in directions:
            if direction not in fetched:
                fetched.add(direction)
                fetch(direction).wait()

    ready(LEAVES[0][0] + LEAVES[0][1])

    @pl.loop(0, SLOTS)
    def _(slot):
        faces = []
        for side in range(2):
            at, row = (16, 15) if side else (0, 0)
            rows = [moved[slot, d, at:at + 16, :].astype(F32)[row:row + 1] for d in LEAVES[0][side]]
            rows.append(sol_ref[slot, at + row:at + row + 1, :])
            rows.append(jnp.zeros((2, CELLS), F32))
            rows = jnp.concatenate(rows, axis=0)
            faces.append(rows)
        xr[slot] = jnp.concatenate(faces, axis=0).astype(BF16)

    faces = xr[...].reshape(SLOTS * 16, CELLS)
    z_low, z_top = dot(faces, pick[0]), dot(faces, pick[1])
    y_low, y_top = dot(faces[:, 0:128], pick_y[0]), dot(faces[:, CELLS - 128:], pick_y[1])
    quarter1 = lane1 >> 5
    ready((15, 16, 17, 18))
    high = slice(CELLS - 128, CELLS)
    lane16 = iota((16, 128), 1)

    def across(d, at, z):
        one = jnp.where(lane16 == z, 1.0, 0.0).astype(BF16)
        tile = moved[:, d, :, at].reshape(SLOTS * S, 128)
        return lax.dot_general(one, tile, (((1,), (1,)), ((), ())), preferred_element_type=F32)

    y_lines = ((across(16, slice(0, 128), 0), across(18, slice(0, 128), S - 1)),
               (across(15, high, 127), across(17, high, 128 - S)))
    for slot in range(SLOTS):
        for side in range(2):
            row = slot * 16 + side * 8
            four = (y_top, y_low, z_top, z_low) if side else (y_low, y_top, z_low, z_top)
            four = [part[row + 1 + i:row + 2 + i] for i, part in enumerate(four)]
            line = jnp.where(quarter1 == 0, four[0], jnp.where(quarter1 == 1, four[1], jnp.where(quarter1 == 2, four[2], four[3])))
            lx[2 * slot + side] = jnp.broadcast_to(line, (16, 128)).astype(BF16)
            tiles = [part[:, 128 * (slot // 4):128 * (slot // 4) + 128] for part in y_lines[side]]
            shift = (128 - S * (slot % 4)) % 128
            if shift:
                tiles[0] = pltpu.roll(tiles[0], shift, 1)
            shift = (shift + S) % 128
            if shift:
                tiles[1] = pltpu.roll(tiles[1], shift, 1)
            ly[2 * slot + side] = jnp.where(lane16 < S, tiles[0], tiles[1]).astype(BF16)

    inv_copy.wait()
    pl.semaphore_wait(barrier, PEERS - 1 + GROUPS - 1)

    def send(src, dst, which, peer):
        return pltpu.make_async_remote_copy(
            src_ref=src.at[peer], dst_ref=dst.at[me], send_sem=send_sem.at[which], recv_sem=recv_sem.at[which],
            device_id={"blk": peer}, device_id_type=pl.DeviceIdType.MESH)

    def all_of(src, dst, which):
        return pltpu.make_async_remote_copy(
            src_ref=src.at[pl.ds(0, PEERS - 1)], dst_ref=dst.at[pl.ds(0, PEERS - 1)], send_sem=send_sem.at[which],
            recv_sem=recv_sem.at[which], device_id={"blk": (me + 1) % PEERS}, device_id_type=pl.DeviceIdType.MESH)

    def grp_copy(src, dst, which, k):
        return pltpu.make_async_remote_copy(
            src_ref=src, dst_ref=dst, send_sem=grp_send.at[which, k], recv_sem=grp_recv.at[which, k],
            device_id={"grp": (grp + k) % GROUPS}, device_id_type=pl.DeviceIdType.MESH)

    def table_copy(k):
        return grp_copy(mine, table_ref.at[k - 1], 0, k)

    def solid_out(k):
        return grp_copy(out_solid.at[k - 1], got_solid.at[k - 1], 1, k)

    def base_out(k):
        return grp_copy(out_base.at[k - 1], got_base.at[k - 1], 3, k)

    def mixed_out(k):
        return grp_copy(out_mixed.at[k - 1], got_mixed.at[k - 1], 2, k)

    upper8 = iota((16, 128), 0) < 8

    @pl.loop(1, PEERS)
    def _(k):
        peer = (me + k) % PEERS
        s1[peer] = jnp.where(upper8, lx[inv[0, peer]].astype(F32), ly[inv[1, peer]].astype(F32)).astype(BF16)
        send(s1, r1, 0, peer).start()

    for k in range(1, GROUPS):
        table_copy(k).start()

    quarter = iota((SLOTS * S, 128), 1) >> 5

    def place_items(into, side, parts, later):
        low = jnp.where(quarter == 0, parts[0], jnp.where(quarter == 1, parts[1], jnp.where(quarter == 2, parts[2], parts[3])))
        late = jnp.where(quarter == later, parts[4], parts[5])
        low, late = low.reshape(SLOTS, S, 128).astype(BF16), late.reshape(SLOTS, S, 128).astype(BF16)
        for slot in range(SLOTS):
            into[2 * slot + side, :, 0:128] = low[slot]
            into[2 * slot + side, :, 128:256] = late[slot]

    sol = sol_ref[...].reshape(SLOTS * S, CELLS).astype(BF16)
    for side in range(2):
        ready(LEAVES[1][side])
        at = high if side else slice(0, 128)
        parts = [dot(moved[:, d, :, at].reshape(SLOTS * S, 128), pick_y[side]) for d in LEAVES[1][side]]
        parts.append(dot(sol[:, at], pick_y[side]))
        place_items(fy, side, parts, 0)
    for side in range(2):
        ready(LEAVES[2][side])
        parts = [dot(moved[:, d].reshape(SLOTS * S, CELLS), pick[side]) for d in LEAVES[2][side]] + [dot(sol, pick[side])]
        place_items(fz, side, parts, 2)

    left = iota((S, 128), 1) < 64

    @pl.loop(1, PEERS)
    def _(k):
        peer = (me + k) % PEERS
        y_part, z_part = fy[inv[1, peer]], fz[inv[2, peer]]
        s2[peer, :, 0:128] = y_part[:, 0:128]
        s2[peer, :, 128:256] = jnp.where(left, y_part[:, 128:].astype(F32), z_part[:, 128:].astype(F32)).astype(BF16)
        s2[peer, :, 256:384] = z_part[:, 0:128]
        send(s2, r2, 1, peer).start()

    row8w, lane8w = iota((8, CELLS), 0), iota((8, CELLS), 1)
    for i, (cy, cz) in enumerate(TURNS):
        hold = lane8w >= 0
        if cy:
            hold = hold & ((lane8w >= S) if cy == 1 else (lane8w < CELLS - S))
        if cz:
            hold = hold & ((lane8w & (S - 1)) != (0 if cz == 1 else S - 1))
        keep[i] = jnp.where(hold, 1.0, 0.0)

    @pl.loop(0, SLOTS)
    def _(slot):
        for side in range(2):
            rows = xr[slot, 8 * side:8 * side + 8, :].astype(F32)
            turned = rows
            for i, d in enumerate(LEAVES[0][side]):
                shift = lane_shift(d)
                if shift:
                    turned = jnp.where(row8w == i, pltpu.roll(rows, shift, 1) * keep[TURNS.index(VELOCITY[d][1:])], turned)
            fx[2 * slot + side] = jnp.concatenate([turned[:, :512], turned[:, 512:]], axis=0).astype(BF16)

    all_of(s1, r1, 0).wait_recv()

    def lines(face, row):
        return jnp.concatenate([r1[owner(slot, face)].astype(F32)[row:row + 1] for slot in range(SLOTS)], axis=0)

    x_lo, x_hi, y_lo, y_hi = lines(0, 0), lines(1, 0), lines(2, 8), lines(3, 8)
    quarter8 = lane8 >> 5
    back = [pltpu.roll(part, 128 - S, 1) for part in (x_lo, x_hi, y_lo, y_hi)]
    x_lo, x_hi = pltpu.roll(x_lo, S, 1), pltpu.roll(x_hi, S, 1)

    def four_of(one, two, three, zero):
        return jnp.where(quarter8 == 1, one, jnp.where(quarter8 == 2, two, jnp.where(quarter8 == 3, three, zero)))

    y_rows = (jnp.where(quarter8 == 1, x_hi, x_lo), jnp.where(quarter8 == 1, x_lo, x_hi))
    z_rows = (four_of(back[1], back[0], back[3], back[2]), four_of(back[0], back[1], back[2], back[3]))
    for slot in range(SLOTS):
        for side in range(2):
            ey[2 * slot + side] = jnp.broadcast_to(y_rows[side][slot:slot + 1], (16, 128))
            ez[2 * slot + side] = jnp.broadcast_to(z_rows[side][slot:slot + 1], (16, 128))
    row16 = iota((16, 128), 0)

    @pl.loop(1, PEERS)
    def _(k):
        peer = (me + k) % PEERS
        part = fx[inv[0, peer]]
        first = jnp.where(row16 == 6, ey[inv[1, peer]], jnp.where(row16 == 7, ez[inv[2, peer]], part[:, 0:128].astype(F32)))
        s3[peer, :, 0:128] = first.astype(BF16)
        s3[peer, :, 128:512] = part[:, 128:512]
        send(s3, r3, 2, peer).start()

    ready((0,))
    solid_copy.wait()
    for k in range(1, GROUPS):
        out_solid[k - 1] = solid_ref[front_slot(k - 1, front, redeal)]
        solid_out(k).start()
    deep, lane = iota((128, CELLS), 0), iota((128, CELLS), 1)
    for side in range(2):
        spread[side] = jnp.where(((deep & (S - 1)) == lane >> 5) & ((lane & (S - 1)) == (S - 1) * side), 1.0, 0.0).astype(BF16)
    row8w = iota((8, CELLS), 0)

    def without_row(block, step):
        if step == 1:
            return jnp.concatenate([jnp.where(row8w == 0, 0.0, block[:8]), block[8:]], axis=0)
        return jnp.concatenate([block[:S - 8], jnp.where(row8w == 7, 0.0, block[S - 8:])], axis=0)

    def masked(block, turn):
        tall = keep[TURNS.index(turn)]
        return block * jnp.concatenate([tall] * 4, axis=0)

    @pl.loop(0, SLOTS)
    def _(slot):
        for d, (step, cy, cz) in enumerate(VELOCITY):
            shift = lane_shift(d)
            if d:
                block = moved[slot, d].astype(F32)
                if step:
                    block = without_row(pltpu.roll(block, step % S, 0), step)
                if shift:
                    block = masked(pltpu.roll(block, shift, 1), (cy, cz))
                moved[slot, d] = block.astype(BF16)
        here = sol_ref[slot]
        below, above = without_row(pltpu.roll(here, 1, 0), 1), without_row(pltpu.roll(here, S - 1, 0), -1)
        total = below + above
        grads[slot, 1] = above - below
        below, above = masked(pltpu.roll(here, S, 1), (1, 0)), masked(pltpu.roll(here, CELLS - S, 1), (-1, 0))
        total = total + below + above
        grads[slot, 2] = above - below
        below, above = masked(pltpu.roll(here, 1, 1), (0, 1)), masked(pltpu.roll(here, CELLS - 1, 1), (0, -1))
        grads[slot, 3] = above - below
        grads[slot, 0] = here + diffusivity * (total + below + above - 6.0 * here)

    for k in range(1, GROUPS):
        out_base[k - 1] = grads[front_slot(k - 1, front, redeal), 0]
        base_out(k).start()
    row32, lane32 = iota((S, 128), 0), iota((S, 128), 1)
    item = lane32 >> 5
    depth32 = lane32 & (S - 1)
    row16w = iota((16, CELLS), 0)
    all_of(s2, r2, 1).wait_recv()

    def shift_rows(plane, down, up):
        from_low = jnp.where(row32 == 0, 0.0, pltpu.roll(plane, 1, 0))
        from_high = jnp.where(row32 == S - 1, 0.0, pltpu.roll(plane, S - 1, 0))
        return jnp.where(item == down, from_low, jnp.where(item == up, from_high, plane))

    @pl.loop(0, SLOTS)
    def _(slot):
        for side in range(2):
            sign = -1.0 if side == 0 else 1.0
            enter = LEAVES[1][1 - side]
            down, up = (1, 2) if side == 0 else (2, 1)
            peer = owner(slot, 2 + side)
            tiles = (shift_rows(r2[peer, :, 0:128].astype(F32), down, up), r2[peer, :, 128:256].astype(F32))
            first = 0 if side == 0 else 128 - S
            at = 0 if side == 0 else CELLS - 128
            for i in range(6):
                cz = VELOCITY[enter[i]][2] if i < 5 else 0
                shift = (first + cz - (i % 4) * S) % 128
                tile = tiles[i // 4]
                if shift:
                    tile = pltpu.roll(tile, shift, 1)
                hit = item == first // S
                if cz:
                    hit = hit & (depth32 != (0 if cz == 1 else S - 1))
                tile = jnp.where(hit, tile, 0.0)
                if i < 5:
                    moved[slot, enter[i], :, at:at + 128] += tile.astype(BF16)
                else:
                    grads[slot, 0, :, at:at + 128] += diffusivity * tile
                    grads[slot, 2, :, at:at + 128] += sign * tile

            enter = LEAVES[2][1 - side]
            peer = owner(slot, 4 + side)
            plane, late = r2[peer, :, 256:384].astype(F32), r2[peer, :, 128:256].astype(F32)
            turn, at3, at4 = (1, 96, 95) if side == 0 else (127, 127, 64)
            turned = jnp.where(lane32 == at3, 0.0, pltpu.roll(plane, turn, 1))
            turned_late = jnp.where(lane32 == at4, 0.0, pltpu.roll(late, 128 - turn, 1))
            plane = jnp.where(item == 3, turned, shift_rows(plane, down, up))
            late = jnp.where(item == 2, turned_late, late)
            stack = [jnp.where(item == i, plane, 0.0).astype(BF16) for i in range(4)]
            stack += [jnp.where(item == i, late, 0.0).astype(BF16) for i in range(2, 4)]
            ghost[...] = dot(jnp.concatenate(stack, axis=0), spread[side])
            for i, d in enumerate(enter):
                moved[slot, d] += ghost[S * i:S * i + S, :].astype(BF16)
            grads[slot, 0] += diffusivity * ghost[5 * S:6 * S, :]
            grads[slot, 3] += sign * ghost[5 * S:6 * S, :]

    all_of(s3, r3, 2).wait_recv()
    item16 = lane16 >> 5

    @pl.loop(0, SLOTS)
    def _(slot):
        for side in range(2):
            edge = r3[owner(slot, 4 + side), :, 0:128].astype(F32)[7:8]
            one, two = (3, 12) if side == 0 else (11, 4)
            hit = ((row16 == one) & (item16 == 1)) | ((row16 == two) & (item16 == 2))
            edge_in[side, slot] = jnp.where(hit, edge, 0.0).astype(BF16)

    z_edges = [dot(edge_in[side].reshape(SLOTS * 16, 128), spread[side]) for side in range(2)]
    edge_rows[...] = (z_edges[0] + z_edges[1]).reshape(SLOTS, 16, CELLS)

    @pl.loop(0, SLOTS)
    def _(slot):
        halves = []
        for side in range(2):
            part = r3[owner(slot, side)].astype(F32)
            halves.append(jnp.concatenate([part[0:8], part[8:16]], axis=1))
        rows = jnp.concatenate(halves, axis=0) + edge_rows[slot]
        low, top = (jnp.broadcast_to(r3[owner(slot, 2 + side), :, 0:128].astype(F32)[6:7], (16, 128)) for side in range(2))
        low = jnp.where(row16 == 1, pltpu.roll(low, 96, 1), jnp.where(row16 == 10, pltpu.roll(low, 64, 1), 0.0))
        top = jnp.where(row16 == 2, pltpu.roll(top, 32, 1), jnp.where(row16 == 9, pltpu.roll(top, 64, 1), 0.0))
        low, top = jnp.where(item16 == 0, low, 0.0), jnp.where(item16 == 3, top, 0.0)
        rows = jnp.concatenate([rows[:, 0:128] + low, rows[:, 128:CELLS - 128], rows[:, CELLS - 128:] + top], axis=1)
        for side in range(2):
            at, hit = (0, row16w == 0) if side == 0 else (16, row16w == 15)
            for i, d in enumerate(LEAVES[0][1 - side]):
                row = rows[8 * side + i:8 * side + i + 1]
                moved[slot, d, at:at + 16, :] += jnp.where(hit, row, 0.0).astype(BF16)
            at, hit, sign = (0, row8w == 0, -1.0) if side == 0 else (S - 8, row8w == 7, 1.0)
            extra = jnp.where(hit, rows[8 * side + 5:8 * side + 6], 0.0)
            grads[slot, 0, at:at + 8, :] += diffusivity * extra
            grads[slot, 1, at:at + 8, :] += sign * extra

            edge = r3[owner(slot, 4 + side), :, 0:128].astype(F32)[7:8]
            third = jnp.sum(jnp.where(lane32 == row32 + 96, edge, 0.0), axis=1, keepdims=True)
            fourth = jnp.sum(jnp.where(lane32 == row32, edge, 0.0), axis=1, keepdims=True)
            third = jnp.where(lane32 == (0 if side == 0 else 127), third, 0.0).astype(BF16)
            fourth = jnp.where(lane32 == (96 if side == 0 else 31), fourth, 0.0).astype(BF16)
            starts, ends = (third, fourth) if side == 0 else (fourth, third)
            moved[slot, 15 if side == 0 else 17, :, 0:128] += starts
            moved[slot, 18 if side == 0 else 16, :, CELLS - 128:] += ends

    def moments(slot, lanes):
        def f(d):
            return moved[slot, d, :, lanes].astype(F32)

        straight, slanted = 0.0, 0.0
        along = [0.0, 0.0, 0.0]
        for d in range(1, 19, 2):
            one, two = f(d), f(d + 1)
            both, diff = one + two, one - two
            if d < 7:
                straight = both + straight
                along[d // 2] = diff + diff
            else:
                slanted = both + slanted
                for axis in range(3):
                    if VELOCITY[d][axis]:
                        along[axis] = along[axis] + diff if VELOCITY[d][axis] == 1 else along[axis] - diff
        density = f(0) * (1.0 / 3.0) + straight * (1.0 / 18.0) + slanted * (1.0 / 36.0)
        over36 = (1.0 / 36.0) / density
        ux, uy, uz = (part * over36 for part in along)
        mixed = grads[slot, 0, :, lanes] - 0.5 * (
            ux * grads[slot, 1, :, lanes] + uy * grads[slot, 2, :, lanes] + uz * grads[slot, 3, :, lanes])
        return density, ux, uy, uz, mixed

    @pl.loop(0, GROUPS - 1)
    def _(step):
        slot = front_slot(step, front, redeal)

        @pl.loop(0, CELLS // WIDE)
        def _(part):
            lanes = pl.ds(pl.multiple_of(part * WIDE, WIDE), WIDE)
            out_mixed[step, :, lanes] = (moments(slot, lanes)[4] - out_base[step, :, lanes]).astype(BF16)

        mixed_out(step + 1).start()

    @pl.loop(0, SLOTS - 3)
    def _(step):
        slot = rest_slot(step, front)

        @pl.loop(0, CELLS // WIDE)
        def _(part):
            lanes = pl.ds(pl.multiple_of(part * WIDE, WIDE), WIDE)
            *now, mixed = moments(slot, lanes)
            for i in range(4):
                flow[step, i, :, lanes] = now[i]
            fresh[step, 0, :, lanes], fresh[step, 1, :, lanes] = react(mixed, solid_ref[slot, :, lanes])

    all_of(s1, r1, 0).wait_send()
    all_of(s2, r2, 1).wait_send()
    all_of(s3, r3, 2).wait_send()
    for k in range(1, GROUPS):
        table_copy(k).wait()
        solid_out(k).wait()
        base_out(k).wait()
        mixed_out(k).wait()


def exchange(populations, solute, solid_fraction, neighbours, front_list, redeal_list):
    vmem, hbm = (pl.BlockSpec(memory_space=m) for m in (pltpu.VMEM, pltpu.HBM))
    operands = (populations, solute, solid_fraction, neighbours, front_list, redeal_list)
    return pl.pallas_call(
        exchange_kernel,
        out_shape=(
            jax.ShapeDtypeStruct(populations.shape, BF16),
            jax.ShapeDtypeStruct((SLOTS - 3, 4, S, CELLS), F32),
            jax.ShapeDtypeStruct((SLOTS - 3, 2, S, CELLS), F32),
            jax.ShapeDtypeStruct((GROUPS - 1, S, CELLS), BF16),
            jax.ShapeDtypeStruct((GROUPS - 1, S, CELLS), F32),
            jax.ShapeDtypeStruct((GROUPS - 1, S, CELLS), F32),
            jax.ShapeDtypeStruct((GROUPS - 1, 1, 128), I32),
        ),
        in_specs=[hbm] * 6,
        out_specs=(vmem,) * 7,
        scratch_shapes=[
            pltpu.VMEM((SLOTS, S, CELLS), F32),
            pltpu.VMEM((SLOTS, S, CELLS), F32),
            pltpu.VMEM((SLOTS, 16, CELLS), BF16),
            pltpu.VMEM((2 * SLOTS, 16, 512), BF16),
            pltpu.VMEM((2 * SLOTS, S, 256), BF16),
            pltpu.VMEM((2 * SLOTS, S, 256), BF16),
            pltpu.VMEM((2 * SLOTS, 16, 128), BF16),
            pltpu.VMEM((2 * SLOTS, 16, 128), BF16),
            pltpu.VMEM((2 * SLOTS, 16, 128), F32),
            pltpu.VMEM((2 * SLOTS, 16, 128), F32),
            pltpu.VMEM((PEERS, 16, 128), BF16),
            pltpu.VMEM((PEERS, S, 384), BF16),
            pltpu.VMEM((PEERS, 16, 512), BF16),
            pltpu.VMEM((PEERS, 16, 128), BF16),
            pltpu.VMEM((PEERS, S, 384), BF16),
            pltpu.VMEM((PEERS, 16, 512), BF16),
            pltpu.VMEM((1, 128), I32),
            pltpu.VMEM((8, 128), I32),
            pltpu.VMEM((len(TURNS), 8, CELLS), F32),
            pltpu.VMEM((2, 128, CELLS), BF16),
            pltpu.VMEM((6 * S, CELLS), F32),
            pltpu.VMEM((SLOTS, 4, S, CELLS), F32),
            pltpu.VMEM((2, SLOTS, 16, 128), BF16),
            pltpu.VMEM((SLOTS, 16, CELLS), F32),
            pltpu.VMEM((GROUPS - 1, S, CELLS), BF16),
            pltpu.VMEM((GROUPS - 1, S, CELLS), F32),
            pltpu.VMEM((GROUPS - 1, S, CELLS), F32),
            pltpu.SMEM((SLOTS, 6), I32),
            pltpu.SMEM((8, 128), I32),
            pltpu.SMEM((3,), I32),
            pltpu.SMEM((3,), I32),
            pltpu.SemaphoreType.DMA((19,)),
            pltpu.SemaphoreType.DMA((6,)),
            pltpu.SemaphoreType.DMA((3,)),
            pltpu.SemaphoreType.DMA((3,)),
            pltpu.SemaphoreType.DMA((4, GROUPS)),
            pltpu.SemaphoreType.DMA((4, GROUPS)),
        ],
        compiler_params=pltpu.CompilerParams(collective_id=0, has_side_effects=True, vmem_limit_bytes=28 * 2**20),
        cost_estimate=pl.CostEstimate(flops=10**9, bytes_accessed=12 * 10**6, transcendentals=0),
        name="exchange",
    )(*(pltpu.with_memory_space_constraint(operand, pltpu.HBM) for operand in operands))


def collide(f, flow, amount, put):
    density, ux, uy, uz = flow
    pair_sum = [f[i] + f[i + 1] for i in range(1, 19, 2)]
    pair_dif = [f[i] - f[i + 1] for i in range(1, 19, 2)]
    share = 1.0 - amount
    scale = (1.0 / relax_time) * share * density
    base = scale - (1.5 * scale) * (ux * ux + uy * uy + uz * uz)
    curve, slope = 4.5 * scale, 3.0 * scale
    rest = (1.0 / relax_time - 1.0) * share
    even_part, odd_part = 0.5 * (amount - rest), 0.5 * (amount + rest)
    put(0, base + (amount - rest) * f[0])
    along_all = (ux, uy, uz, ux + uy, ux - uy, ux + uz, ux - uz, uy + uz, uy - uz)
    for pair in range(9):
        along = along_all[pair]
        even = base + (curve * along) * along + even_part * pair_sum[pair]
        odd = slope * along - odd_part * pair_dif[pair]
        put(2 * pair + 1, even + odd)
        put(2 * pair + 2, even - odd)


def collide_kernel(front, table, moved, flow, fresh, got_mixed, got_base, got_solid, solid, new_pop, new_sol, new_solid,
                   ones, done, placed, sems, pop_sems):
    ones[...] = jnp.ones(ones.shape, BF16)
    copies = []
    for k in range(3):
        slot = place_slot(k, front, table)
        placed[0, k], placed[1, k] = react(got_base[k] + got_mixed[k].astype(F32), got_solid[k])
        copies.append(pltpu.make_async_copy(ones, new_pop.at[slot], sems.at[0, k]))
        copies.append(pltpu.make_async_copy(placed.at[0, k], new_sol.at[slot], sems.at[1, k]))
        copies.append(pltpu.make_async_copy(placed.at[1, k], new_solid.at[slot], sems.at[2, k]))
    for k in range(SLOTS - 3):
        slot = rest_slot(k, front)
        copies.append(pltpu.make_async_copy(fresh.at[k, 0], new_sol.at[slot], sems.at[1, 3 + k]))
        copies.append(pltpu.make_async_copy(fresh.at[k, 1], new_solid.at[slot], sems.at[2, 3 + k]))
    for copy in copies:
        copy.start()

    def out(index):
        return pltpu.make_async_copy(done.at[index], new_pop.at[rest_slot(index, front)], pop_sems.at[index])

    @pl.loop(0, SLOTS - 3)
    def _(index):
        slot = rest_slot(index, front)
        for row in range(0, S, 16):
            for lane in range(0, CELLS, 128):
                rows, lanes = slice(row, row + 16), slice(lane, lane + 128)

                def put(direction, value):
                    done[index, direction, rows, lanes] = value.astype(BF16)

                f = [moved[slot, d, rows, lanes].astype(F32) for d in range(19)]
                collide(f, [flow[index, i, rows, lanes] for i in range(4)], solid[slot, rows, lanes], put)
        out(index).start()

    for copy in copies:
        copy.wait()
    for index in range(SLOTS - 3):
        out(index).wait()


def collide_all(front, table, moved, flow, fresh, got_mixed, got_base, got_solid, solid_fraction):
    smem, vmem, anywhere = (pl.BlockSpec(memory_space=m) for m in (pltpu.SMEM, pltpu.VMEM, pl.ANY))
    return pl.pallas_call(
        collide_kernel,
        out_shape=(
            jax.ShapeDtypeStruct(moved.shape, BF16),
            jax.ShapeDtypeStruct(solid_fraction.shape, F32),
            jax.ShapeDtypeStruct(solid_fraction.shape, F32),
        ),
        in_specs=[smem] * 2 + [vmem] * 7,
        out_specs=(anywhere,) * 3,
        scratch_shapes=[
            pltpu.VMEM((19, S, CELLS), BF16),
            pltpu.VMEM((SLOTS - 3, 19, S, CELLS), BF16),
            pltpu.VMEM((2, 3, S, CELLS), F32),
            pltpu.SemaphoreType.DMA((3, SLOTS)),
            pltpu.SemaphoreType.DMA((SLOTS - 3,)),
        ],
        compiler_params=pltpu.CompilerParams(vmem_limit_bytes=16 * 2**20),
        cost_estimate=pl.CostEstimate(flops=10**8, bytes_accessed=16 * 10**6, transcendentals=0),
        name="collide",
    )(front, table, moved, flow, fresh, got_mixed, got_base, got_solid, solid_fraction)


def body(populations, solute, solid_fraction, neighbours, front_list, redeal_list):
    moved, flow, fresh, got_mixed, got_base, got_solid, table = exchange(
        populations, solute, solid_fraction, neighbours, front_list, redeal_list)
    return collide_all(front_list, table, moved, flow, fresh, got_mixed, got_base, got_solid, solid_fraction)


def solution(mesh):
    deal = ("blk", "grp")
    return jax.shard_map(
        body,
        mesh=mesh,
        in_specs=(P(deal, None, None, None), P(deal, None, None), P(deal, None, None), P(deal, None), P(deal), P(deal)),
        out_specs=(P(deal, None, None, None), P(deal, None, None), P(deal, None, None)),
        check_vma=False,
    )
```

```python
import jax
import jax.numpy as jnp
from jax import lax
from jax.experimental import pallas as pl
from jax.experimental.pallas import tpu as pltpu
from jax.sharding import PartitionSpec as P

VELOCITY = (
    (0, 0, 0), (1, 0, 0), (-1, 0, 0), (0, 1, 0), (0, -1, 0), (0, 0, 1), (0, 0, -1),
    (1, 1, 0), (-1, -1, 0), (1, -1, 0), (-1, 1, 0), (1, 0, 1), (-1, 0, -1), (1, 0, -1),
    (-1, 0, 1), (0, 1, 1), (0, -1, -1), (0, 1, -1), (0, -1, 1),
)
LEAVES = (
    ((2, 8, 10, 12, 14), (1, 7, 9, 11, 13)),
    ((4, 8, 9, 16, 18), (3, 7, 10, 15, 17)),
    ((6, 12, 13, 16, 17), (5, 11, 14, 15, 18)),
)
FETCH = (2, 8, 10, 12, 14, 1, 7, 9, 11, 13, 15, 16, 17, 18, 3, 4, 6, 5, 0)
SLOTS = 8
S = 32
CELLS = S * S
PEERS = 32
GROUPS = 4
TURNS = ((0, 1), (0, -1), (1, 0), (-1, 0), (1, 1), (-1, -1), (1, -1), (-1, 1))
WIDE = 256
F32, BF16, I32 = jnp.float32, jnp.bfloat16, jnp.int32
relax_time = 0.8
diffusivity = 0.1
rate_const = 0.5
saturation = 1.0


def iota(shape, dim):
    return lax.broadcasted_iota(I32, shape, dim)


def lane_shift(direction):
    return (S * VELOCITY[direction][1] + VELOCITY[direction][2]) % CELLS


def dot(a, b):
    return jnp.dot(a, b, preferred_element_type=F32)


def react(mixed, amount):
    reaction = rate_const * amount * (1.0 - amount) * (saturation - mixed)
    return mixed + reaction, amount - reaction


def front_slot(step, front, redeal):
    group = (front[0] >> 3) & (GROUPS - 1)
    slot = front[0] & (SLOTS - 1)
    for entry in range(1, 3):
        ahead = ((redeal[entry] >> 3) - group) & (GROUPS - 1)
        slot = jnp.where(ahead == step + 1, front[entry] & (SLOTS - 1), slot)
    return slot


def rest_slot(step, front):
    a, b, c = (front[entry] & (SLOTS - 1) for entry in range(3))
    low, high = jnp.minimum(a, b), jnp.maximum(a, b)
    mid, high = jnp.minimum(high, c), jnp.maximum(high, c)
    low, mid = jnp.minimum(low, mid), jnp.maximum(low, mid)
    slot = step
    for taken in (low, mid, high):
        slot = slot + jnp.where(slot >= taken, 1, 0)
    return slot


def place_slot(step, front, table):
    group = (front[0] >> 3) & (GROUPS - 1)
    slot = table[step, 0, 0] & (SLOTS - 1)
    for entry in range(1, 3):
        place = table[step, 0, entry]
        slot = jnp.where((place >> 3) & (GROUPS - 1) == group, place & (SLOTS - 1), slot)
    return slot


def exchange_kernel(pop_hbm, sol_hbm, solid_hbm, nbr_hbm, front_hbm, redeal_hbm,
                    done, fresh, got_mixed, got_base, got_solid, table_ref,
                    moved, flow, sol_ref, solid_ref, xr, fx, fy, fz, lx, ly, ey, ez, s1, s2, s3, s4, r1, r2, r3, r4, mine, inv_vmem,
                    keep, spread, ghost, grads, edge_in, edge_rows, out_mixed, out_base, out_solid,
                    nbr, inv, front, redeal, fetch_sem, small_sem, send_sem, recv_sem, grp_send, grp_recv):
    me = lax.axis_index("blk")
    grp = lax.axis_index("grp")

    def fetch(direction):
        return pltpu.make_async_copy(pop_hbm.at[:, direction], moved.at[:, direction], fetch_sem.at[direction])

    nbr_copy = pltpu.make_async_copy(nbr_hbm, nbr, small_sem.at[0])
    redeal_copy = pltpu.make_async_copy(redeal_hbm, redeal, small_sem.at[1])
    inv_copy = pltpu.make_async_copy(inv_vmem, inv, small_sem.at[2])
    sol_copy = pltpu.make_async_copy(sol_hbm, sol_ref, small_sem.at[3])
    front_copy = pltpu.make_async_copy(front_hbm, front, small_sem.at[4])
    solid_copy = pltpu.make_async_copy(solid_hbm, solid_ref, small_sem.at[5])
    nbr_copy.start()
    redeal_copy.start()
    front_copy.start()
    sol_copy.start()
    for direction in FETCH:
        fetch(direction).start()

    solid_copy.start()
    barrier = pltpu.get_barrier_semaphore()

    @pl.loop(1, PEERS)
    def _(k):
        pl.semaphore_signal(barrier, inc=1, device_id={"blk": (me + k) % PEERS}, device_id_type=pl.DeviceIdType.MESH)

    for k in range(1, GROUPS):
        pl.semaphore_signal(barrier, inc=1, device_id={"grp": (grp + k) % GROUPS}, device_id_type=pl.DeviceIdType.MESH)

    deep, lane = iota((CELLS, 128), 0), iota((CELLS, 128), 1) & (S - 1)
    pick = [jnp.where(deep == lane * S + z, 1.0, 0.0).astype(BF16) for z in (0, S - 1)]
    wide, lane = iota((128, 128), 0), iota((128, 128), 1) & (S - 1)
    pick_y = [jnp.where(wide == lane + first, 1.0, 0.0).astype(BF16) for first in (0, 128 - S)]

    nbr_copy.wait()
    redeal_copy.wait()
    front_copy.wait()

    def owner(slot, face):
        return nbr[slot, face] >> 5

    row8, lane8 = iota((8, 128), 0), iota((8, 128), 1)
    found = jnp.zeros((8, 128), I32)
    for axis in range(3):
        hit = jnp.zeros((8, 128), I32)
        for slot in range(SLOTS):
            for side in range(2):
                hit = jnp.where(lane8 == owner(slot, 2 * axis + side), 2 * slot + side, hit)
        found = jnp.where(row8 == axis, hit, found)
    inv_vmem[...] = found
    inv_copy.start()
    lane1 = iota((1, 128), 1)
    mine[...] = jnp.where(lane1 == 0, redeal[0], jnp.where(lane1 == 1, redeal[1], redeal[2]))
    sol_copy.wait()

    fetched = set()

    def ready(directions):
        for direction in directions:
            if direction not in fetched:
                fetched.add(direction)
                fetch(direction).wait()

    high = slice(CELLS - 128, CELLS)
    ready(LEAVES[0][0] + LEAVES[0][1])

    @pl.loop(0, SLOTS)
    def _(slot):
        faces = []
        for side in range(2):
            at, row = (16, 15) if side else (0, 0)
            rows = [moved[slot, d, at:at + 16, :].astype(F32)[row:row + 1] for d in LEAVES[0][side]]
            rows.append(sol_ref[slot, at + row:at + row + 1, :])
            rows.append(jnp.zeros((2, CELLS), F32))
            rows = jnp.concatenate(rows, axis=0)
            faces.append(rows)
        xr[slot] = jnp.concatenate(faces, axis=0).astype(BF16)

    faces = xr[...].reshape(SLOTS * 16, CELLS)
    z_low, z_top = dot(faces, pick[0]), dot(faces, pick[1])
    y_low, y_top = dot(faces[:, 0:128], pick_y[0]), dot(faces[:, CELLS - 128:], pick_y[1])
    quarter1 = lane1 >> 5
    ready((15, 16, 17, 18))
    lane16 = iota((16, 128), 1)

    def across(d, at, z):
        one = jnp.where(lane16 == z, 1.0, 0.0).astype(BF16)
        tile = moved[:, d, :, at].reshape(SLOTS * S, 128)
        return lax.dot_general(one, tile, (((1,), (1,)), ((), ())), preferred_element_type=F32)

    y_lines = ((across(16, slice(0, 128), 0), across(18, slice(0, 128), S - 1)),
               (across(15, high, 127), across(17, high, 128 - S)))
    for slot in range(SLOTS):
        for side in range(2):
            row = slot * 16 + side * 8
            four = (y_top, y_low, z_top, z_low) if side else (y_low, y_top, z_low, z_top)
            four = [part[row + 1 + i:row + 2 + i] for i, part in enumerate(four)]
            line = jnp.where(quarter1 == 0, four[0], jnp.where(quarter1 == 1, four[1], jnp.where(quarter1 == 2, four[2], four[3])))
            lx[2 * slot + side] = line
            tiles = [part[:, 128 * (slot // 4):128 * (slot // 4) + 128] for part in y_lines[side]]
            shift = (128 - S * (slot % 4)) % 128
            if shift:
                tiles[0] = pltpu.roll(tiles[0], shift, 1)
            shift = (shift + S) % 128
            if shift:
                tiles[1] = pltpu.roll(tiles[1], shift, 1)
            ly[2 * slot + side] = jnp.where(lane16 < S, tiles[0], tiles[1])[0:1]

    inv_copy.wait()
    pl.semaphore_wait(barrier, PEERS - 1 + GROUPS - 1)

    def send(src, dst, which, peer):
        return pltpu.make_async_remote_copy(
            src_ref=src.at[peer], dst_ref=dst.at[me], send_sem=send_sem.at[which], recv_sem=recv_sem.at[which],
            device_id={"blk": peer}, device_id_type=pl.DeviceIdType.MESH)

    def all_of(src, dst, which):
        return pltpu.make_async_remote_copy(
            src_ref=src.at[pl.ds(0, PEERS - 1)], dst_ref=dst.at[pl.ds(0, PEERS - 1)], send_sem=send_sem.at[which],
            recv_sem=recv_sem.at[which], device_id={"blk": (me + 1) % PEERS}, device_id_type=pl.DeviceIdType.MESH)

    def grp_copy(src, dst, which, k):
        return pltpu.make_async_remote_copy(
            src_ref=src, dst_ref=dst, send_sem=grp_send.at[which, k], recv_sem=grp_recv.at[which, k],
            device_id={"grp": (grp + k) % GROUPS}, device_id_type=pl.DeviceIdType.MESH)

    def table_copy(k):
        return grp_copy(mine, table_ref.at[k - 1], 0, k)

    def solid_out(k):
        return grp_copy(out_solid.at[k - 1], got_solid.at[k - 1], 1, k)

    def base_out(k):
        return grp_copy(out_base.at[k - 1], got_base.at[k - 1], 3, k)

    def mixed_out(k):
        return grp_copy(out_mixed.at[k - 1], got_mixed.at[k - 1], 2, k)

    @pl.loop(1, PEERS)
    def _(k):
        peer = (me + k) % PEERS
        s1[peer, :, 0:128] = lx[inv[0, peer]]
        s1[peer, :, 128:256] = ly[inv[1, peer]]
        send(s1, r1, 0, peer).start()

    for k in range(1, GROUPS):
        table_copy(k).start()

    quarter = iota((SLOTS * S, 128), 1) >> 5

    def place_items(into, side, parts, later):
        low = jnp.where(quarter == 0, parts[0], jnp.where(quarter == 1, parts[1], jnp.where(quarter == 2, parts[2], parts[3])))
        late = jnp.where(quarter == later, parts[4], parts[5])
        low, late = low.reshape(SLOTS, S, 128).astype(BF16), late.reshape(SLOTS, S, 128).astype(BF16)
        for slot in range(SLOTS):
            into[2 * slot + side, :, 0:128] = low[slot]
            into[2 * slot + side, :, 128:256] = late[slot]

    sol = sol_ref[...].reshape(SLOTS * S, CELLS).astype(BF16)
    for side in range(2):
        ready(LEAVES[1][side])
        at = high if side else slice(0, 128)
        parts = [dot(moved[:, d, :, at].reshape(SLOTS * S, 128), pick_y[side]) for d in LEAVES[1][side]]
        parts.append(dot(sol[:, at], pick_y[side]))
        place_items(fy, side, parts, 0)
    for side in range(2):
        ready(LEAVES[2][side])
        parts = [dot(moved[:, d].reshape(SLOTS * S, CELLS), pick[side]) for d in LEAVES[2][side]] + [dot(sol, pick[side])]
        place_items(fz, side, parts, 2)

    left = iota((S, 128), 1) < 64

    @pl.loop(1, PEERS)
    def _(k):
        peer = (me + k) % PEERS
        y_part, z_part = fy[inv[1, peer]], fz[inv[2, peer]]
        s2[peer, :, 0:128] = y_part[:, 0:128]
        s2[peer, :, 128:256] = jnp.where(left, y_part[:, 128:].astype(F32), z_part[:, 128:].astype(F32)).astype(BF16)
        s2[peer, :, 256:384] = z_part[:, 0:128]
        send(s2, r2, 1, peer).start()

    row8w, lane8w = iota((8, CELLS), 0), iota((8, CELLS), 1)
    for i, (cy, cz) in enumerate(TURNS):
        hold = lane8w >= 0
        if cy:
            hold = hold & ((lane8w >= S) if cy == 1 else (lane8w < CELLS - S))
        if cz:
            hold = hold & ((lane8w & (S - 1)) != (0 if cz == 1 else S - 1))
        keep[i] = jnp.where(hold, 1.0, 0.0)

    @pl.loop(0, SLOTS)
    def _(slot):
        for side in range(2):
            rows = xr[slot, 8 * side:8 * side + 8, :].astype(F32)
            turned = rows
            for i, d in enumerate(LEAVES[0][side]):
                shift = lane_shift(d)
                if shift:
                    turned = jnp.where(row8w == i, pltpu.roll(rows, shift, 1) * keep[TURNS.index(VELOCITY[d][1:])], turned)
            fx[2 * slot + side] = jnp.concatenate([turned[:, :512], turned[:, 512:]], axis=0).astype(BF16)

    all_of(s1, r1, 0).wait_recv()

    def lines(face, at):
        return jnp.concatenate([r1[owner(slot, face), :, at:at + 128] for slot in range(SLOTS)], axis=0)

    x_lo, x_hi, y_lo, y_hi = lines(0, 0), lines(1, 0), lines(2, 128), lines(3, 128)
    quarter8 = lane8 >> 5
    back = [pltpu.roll(part, 128 - S, 1) for part in (x_lo, x_hi, y_lo, y_hi)]
    x_lo, x_hi = pltpu.roll(x_lo, S, 1), pltpu.roll(x_hi, S, 1)

    def four_of(one, two, three, zero):
        return jnp.where(quarter8 == 1, one, jnp.where(quarter8 == 2, two, jnp.where(quarter8 == 3, three, zero)))

    y_rows = (jnp.where(quarter8 == 1, x_hi, x_lo), jnp.where(quarter8 == 1, x_lo, x_hi))
    z_rows = (four_of(back[1], back[0], back[3], back[2]), four_of(back[0], back[1], back[2], back[3]))
    for slot in range(SLOTS):
        for side in range(2):
            ey[2 * slot + side] = y_rows[side][slot:slot + 1]
            ez[2 * slot + side] = z_rows[side][slot:slot + 1]
    row16 = iota((16, 128), 0)

    @pl.loop(1, PEERS)
    def _(k):
        peer = (me + k) % PEERS
        s4[peer, :, 0:128] = ey[inv[1, peer]]
        s4[peer, :, 128:256] = ez[inv[2, peer]]
        send(s4, r4, 3, peer).start()

    @pl.loop(1, PEERS)
    def _(k):
        peer = (me + k) % PEERS
        s3[peer] = fx[inv[0, peer]]
        send(s3, r3, 2, peer).start()

    ready((0,))
    solid_copy.wait()
    for k in range(1, GROUPS):
        out_solid[k - 1] = solid_ref[front_slot(k - 1, front, redeal)]
        solid_out(k).start()
    deep, lane = iota((128, CELLS), 0), iota((128, CELLS), 1)
    for side in range(2):
        spread[side] = jnp.where(((deep & (S - 1)) == lane >> 5) & ((lane & (S - 1)) == (S - 1) * side), 1.0, 0.0).astype(BF16)
    row8w = iota((8, CELLS), 0)

    def without_row(block, step):
        if step == 1:
            return jnp.concatenate([jnp.where(row8w == 0, 0.0, block[:8]), block[8:]], axis=0)
        return jnp.concatenate([block[:S - 8], jnp.where(row8w == 7, 0.0, block[S - 8:])], axis=0)

    def masked(block, turn):
        tall = keep[TURNS.index(turn)]
        return block * jnp.concatenate([tall] * 4, axis=0)

    @pl.loop(0, SLOTS)
    def _(slot):
        for d, (step, cy, cz) in enumerate(VELOCITY):
            shift = lane_shift(d)
            if d:
                block = moved[slot, d].astype(F32)
                if step:
                    block = without_row(pltpu.roll(block, step % S, 0), step)
                if shift:
                    block = masked(pltpu.roll(block, shift, 1), (cy, cz))
                moved[slot, d] = block.astype(BF16)
        here = sol_ref[slot]
        below, above = without_row(pltpu.roll(here, 1, 0), 1), without_row(pltpu.roll(here, S - 1, 0), -1)
        total = below + above
        grads[slot, 1] = above - below
        below, above = masked(pltpu.roll(here, S, 1), (1, 0)), masked(pltpu.roll(here, CELLS - S, 1), (-1, 0))
        total = total + below + above
        grads[slot, 2] = above - below
        below, above = masked(pltpu.roll(here, 1, 1), (0, 1)), masked(pltpu.roll(here, CELLS - 1, 1), (0, -1))
        grads[slot, 3] = above - below
        grads[slot, 0] = here + diffusivity * (total + below + above - 6.0 * here)

    for k in range(1, GROUPS):
        out_base[k - 1] = grads[front_slot(k - 1, front, redeal), 0]
        base_out(k).start()
    row32, lane32 = iota((S, 128), 0), iota((S, 128), 1)
    item = lane32 >> 5
    depth32 = lane32 & (S - 1)
    row16w = iota((16, CELLS), 0)
    all_of(s2, r2, 1).wait_recv()

    def shift_rows(plane, down, up):
        from_low = jnp.where(row32 == 0, 0.0, pltpu.roll(plane, 1, 0))
        from_high = jnp.where(row32 == S - 1, 0.0, pltpu.roll(plane, S - 1, 0))
        return jnp.where(item == down, from_low, jnp.where(item == up, from_high, plane))

    @pl.loop(0, SLOTS)
    def _(slot):
        for side in range(2):
            sign = -1.0 if side == 0 else 1.0
            enter = LEAVES[1][1 - side]
            down, up = (1, 2) if side == 0 else (2, 1)
            peer = owner(slot, 2 + side)
            tiles = (shift_rows(r2[peer, :, 0:128].astype(F32), down, up), r2[peer, :, 128:256].astype(F32))
            first = 0 if side == 0 else 128 - S
            at = 0 if side == 0 else CELLS - 128
            for i in range(6):
                cz = VELOCITY[enter[i]][2] if i < 5 else 0
                shift = (first + cz - (i % 4) * S) % 128
                tile = tiles[i // 4]
                if shift:
                    tile = pltpu.roll(tile, shift, 1)
                hit = item == first // S
                if cz:
                    hit = hit & (depth32 != (0 if cz == 1 else S - 1))
                tile = jnp.where(hit, tile, 0.0)
                if i < 5:
                    moved[slot, enter[i], :, at:at + 128] += tile.astype(BF16)
                else:
                    grads[slot, 0, :, at:at + 128] += diffusivity * tile
                    grads[slot, 2, :, at:at + 128] += sign * tile

            enter = LEAVES[2][1 - side]
            peer = owner(slot, 4 + side)
            plane, late = r2[peer, :, 256:384].astype(F32), r2[peer, :, 128:256].astype(F32)
            turn, at3, at4 = (1, 96, 95) if side == 0 else (127, 127, 64)
            turned = jnp.where(lane32 == at3, 0.0, pltpu.roll(plane, turn, 1))
            turned_late = jnp.where(lane32 == at4, 0.0, pltpu.roll(late, 128 - turn, 1))
            plane = jnp.where(item == 3, turned, shift_rows(plane, down, up))
            late = jnp.where(item == 2, turned_late, late)
            stack = [jnp.where(item == i, plane, 0.0).astype(BF16) for i in range(4)]
            stack += [jnp.where(item == i, late, 0.0).astype(BF16) for i in range(2, 4)]
            ghost[...] = dot(jnp.concatenate(stack, axis=0), spread[side])
            for i, d in enumerate(enter):
                moved[slot, d] += ghost[S * i:S * i + S, :].astype(BF16)
            grads[slot, 0] += diffusivity * ghost[5 * S:6 * S, :]
            grads[slot, 3] += sign * ghost[5 * S:6 * S, :]

    all_of(s3, r3, 2).wait_recv()
    all_of(s4, r4, 3).wait_recv()
    item16 = lane16 >> 5

    @pl.loop(0, SLOTS)
    def _(slot):
        for side in range(2):
            edge = r4[owner(slot, 4 + side), :, 128:256]
            one, two = (3, 12) if side == 0 else (11, 4)
            hit = ((row16 == one) & (item16 == 1)) | ((row16 == two) & (item16 == 2))
            edge_in[side, slot] = jnp.where(hit, edge, 0.0).astype(BF16)

    z_edges = [dot(edge_in[side].reshape(SLOTS * 16, 128), spread[side]) for side in range(2)]
    edge_rows[...] = (z_edges[0] + z_edges[1]).reshape(SLOTS, 16, CELLS)

    @pl.loop(0, SLOTS)
    def _(slot):
        halves = []
        for side in range(2):
            part = r3[owner(slot, side)].astype(F32)
            halves.append(jnp.concatenate([part[0:8], part[8:16]], axis=1))
        rows = jnp.concatenate(halves, axis=0) + edge_rows[slot]
        low, top = (jnp.broadcast_to(r4[owner(slot, 2 + side), :, 0:128], (16, 128)) for side in range(2))
        low = jnp.where(row16 == 1, pltpu.roll(low, 96, 1), jnp.where(row16 == 10, pltpu.roll(low, 64, 1), 0.0))
        top = jnp.where(row16 == 2, pltpu.roll(top, 32, 1), jnp.where(row16 == 9, pltpu.roll(top, 64, 1), 0.0))
        low, top = jnp.where(item16 == 0, low, 0.0), jnp.where(item16 == 3, top, 0.0)
        rows = jnp.concatenate([rows[:, 0:128] + low, rows[:, 128:CELLS - 128], rows[:, CELLS - 128:] + top], axis=1)
        for side in range(2):
            at, hit = (0, row16w == 0) if side == 0 else (16, row16w == 15)
            for i, d in enumerate(LEAVES[0][1 - side]):
                row = rows[8 * side + i:8 * side + i + 1]
                moved[slot, d, at:at + 16, :] += jnp.where(hit, row, 0.0).astype(BF16)
            at, hit, sign = (0, row8w == 0, -1.0) if side == 0 else (S - 8, row8w == 7, 1.0)
            extra = jnp.where(hit, rows[8 * side + 5:8 * side + 6], 0.0)
            grads[slot, 0, at:at + 8, :] += diffusivity * extra
            grads[slot, 1, at:at + 8, :] += sign * extra

            edge = r4[owner(slot, 4 + side), :, 128:256]
            third = jnp.sum(jnp.where(lane32 == row32 + 96, edge, 0.0), axis=1, keepdims=True)
            fourth = jnp.sum(jnp.where(lane32 == row32, edge, 0.0), axis=1, keepdims=True)
            third = jnp.where(lane32 == (0 if side == 0 else 127), third, 0.0).astype(BF16)
            fourth = jnp.where(lane32 == (96 if side == 0 else 31), fourth, 0.0).astype(BF16)
            starts, ends = (third, fourth) if side == 0 else (fourth, third)
            moved[slot, 15 if side == 0 else 17, :, 0:128] += starts
            moved[slot, 18 if side == 0 else 16, :, CELLS - 128:] += ends

    def moments(slot, lanes):
        def f(d):
            return moved[slot, d, :, lanes].astype(F32)

        straight, slanted = 0.0, 0.0
        along = [0.0, 0.0, 0.0]
        for d in range(1, 19, 2):
            one, two = f(d), f(d + 1)
            both, diff = one + two, one - two
            if d < 7:
                straight = both + straight
                along[d // 2] = diff + diff
            else:
                slanted = both + slanted
                for axis in range(3):
                    if VELOCITY[d][axis]:
                        along[axis] = along[axis] + diff if VELOCITY[d][axis] == 1 else along[axis] - diff
        density = f(0) * (1.0 / 3.0) + straight * (1.0 / 18.0) + slanted * (1.0 / 36.0)
        over36 = (1.0 / 36.0) / density
        ux, uy, uz = (part * over36 for part in along)
        mixed = grads[slot, 0, :, lanes] - 0.5 * (
            ux * grads[slot, 1, :, lanes] + uy * grads[slot, 2, :, lanes] + uz * grads[slot, 3, :, lanes])
        return density, ux, uy, uz, mixed

    @pl.loop(0, GROUPS - 1)
    def _(step):
        slot = front_slot(step, front, redeal)

        @pl.loop(0, CELLS // WIDE)
        def _(part):
            lanes = pl.ds(pl.multiple_of(part * WIDE, WIDE), WIDE)
            out_mixed[step, :, lanes] = (moments(slot, lanes)[4] - out_base[step, :, lanes]).astype(BF16)

        mixed_out(step + 1).start()

    @pl.loop(0, SLOTS - 3)
    def _(step):
        slot = rest_slot(step, front)

        @pl.loop(0, CELLS // WIDE)
        def _(part):
            lanes = pl.ds(pl.multiple_of(part * WIDE, WIDE), WIDE)
            *now, mixed = moments(slot, lanes)
            for i in range(4):
                flow[step, i, :, lanes] = now[i]
            fresh[step, 0, :, lanes], fresh[step, 1, :, lanes] = react(mixed, solid_ref[slot, :, lanes])

    @pl.loop(0, SLOTS - 3)
    def _(index):
        slot = rest_slot(index, front)

        @pl.loop(0, CELLS // 128)
        def _(part):
            lanes = pl.ds(pl.multiple_of(part * 128, 128), 128)
            for row in range(0, S, 16):
                rows = slice(row, row + 16)

                def put(direction, value):
                    done[index, direction, rows, lanes] = value.astype(BF16)

                f = [moved[slot, d, rows, lanes].astype(F32) for d in range(19)]
                collide(f, [flow[index, i, rows, lanes] for i in range(4)], solid_ref[slot, rows, lanes], put)

    all_of(s1, r1, 0).wait_send()
    all_of(s2, r2, 1).wait_send()
    all_of(s3, r3, 2).wait_send()
    all_of(s4, r4, 3).wait_send()
    for k in range(1, GROUPS):
        table_copy(k).wait()
        solid_out(k).wait()
        base_out(k).wait()
        mixed_out(k).wait()


def exchange(populations, solute, solid_fraction, neighbours, front_list, redeal_list):
    vmem, hbm = (pl.BlockSpec(memory_space=m) for m in (pltpu.VMEM, pltpu.HBM))
    operands = (populations, solute, solid_fraction, neighbours, front_list, redeal_list)
    return pl.pallas_call(
        exchange_kernel,
        out_shape=(
            jax.ShapeDtypeStruct((SLOTS - 3, 19, S, CELLS), BF16),
            jax.ShapeDtypeStruct((SLOTS - 3, 2, S, CELLS), F32),
            jax.ShapeDtypeStruct((GROUPS - 1, S, CELLS), BF16),
            jax.ShapeDtypeStruct((GROUPS - 1, S, CELLS), F32),
            jax.ShapeDtypeStruct((GROUPS - 1, S, CELLS), F32),
            jax.ShapeDtypeStruct((GROUPS - 1, 1, 128), I32),
        ),
        in_specs=[hbm] * 6,
        out_specs=(vmem,) * 6,
        scratch_shapes=[
            pltpu.VMEM((SLOTS, 19, S, CELLS), BF16),
            pltpu.VMEM((SLOTS - 3, 4, S, CELLS), F32),
            pltpu.VMEM((SLOTS, S, CELLS), F32),
            pltpu.VMEM((SLOTS, S, CELLS), F32),
            pltpu.VMEM((SLOTS, 16, CELLS), BF16),
            pltpu.VMEM((2 * SLOTS, 16, 512), BF16),
            pltpu.VMEM((2 * SLOTS, S, 256), BF16),
            pltpu.VMEM((2 * SLOTS, S, 256), BF16),
            pltpu.VMEM((2 * SLOTS, 1, 128), F32),
            pltpu.VMEM((2 * SLOTS, 1, 128), F32),
            pltpu.VMEM((2 * SLOTS, 1, 128), F32),
            pltpu.VMEM((2 * SLOTS, 1, 128), F32),
            pltpu.VMEM((PEERS, 1, 256), F32),
            pltpu.VMEM((PEERS, S, 384), BF16),
            pltpu.VMEM((PEERS, 16, 512), BF16),
            pltpu.VMEM((PEERS, 1, 256), F32),
            pltpu.VMEM((PEERS, 1, 256), F32),
            pltpu.VMEM((PEERS, S, 384), BF16),
            pltpu.VMEM((PEERS, 16, 512), BF16),
            pltpu.VMEM((PEERS, 1, 256), F32),
            pltpu.VMEM((1, 128), I32),
            pltpu.VMEM((8, 128), I32),
            pltpu.VMEM((len(TURNS), 8, CELLS), F32),
            pltpu.VMEM((2, 128, CELLS), BF16),
            pltpu.VMEM((6 * S, CELLS), F32),
            pltpu.VMEM((SLOTS, 4, S, CELLS), F32),
            pltpu.VMEM((2, SLOTS, 16, 128), BF16),
            pltpu.VMEM((SLOTS, 16, CELLS), F32),
            pltpu.VMEM((GROUPS - 1, S, CELLS), BF16),
            pltpu.VMEM((GROUPS - 1, S, CELLS), F32),
            pltpu.VMEM((GROUPS - 1, S, CELLS), F32),
            pltpu.SMEM((SLOTS, 6), I32),
            pltpu.SMEM((8, 128), I32),
            pltpu.SMEM((3,), I32),
            pltpu.SMEM((3,), I32),
            pltpu.SemaphoreType.DMA((19,)),
            pltpu.SemaphoreType.DMA((6,)),
            pltpu.SemaphoreType.DMA((4,)),
            pltpu.SemaphoreType.DMA((4,)),
            pltpu.SemaphoreType.DMA((4, GROUPS)),
            pltpu.SemaphoreType.DMA((4, GROUPS)),
        ],
        compiler_params=pltpu.CompilerParams(collective_id=0, has_side_effects=True, vmem_limit_bytes=44 * 2**20),
        cost_estimate=pl.CostEstimate(flops=10**9, bytes_accessed=12 * 10**6, transcendentals=0),
        name="exchange",
    )(*(pltpu.with_memory_space_constraint(operand, pltpu.HBM) for operand in operands))


def collide(f, flow, amount, put):
    density, ux, uy, uz = flow
    pair_sum = [f[i] + f[i + 1] for i in range(1, 19, 2)]
    pair_dif = [f[i] - f[i + 1] for i in range(1, 19, 2)]
    share = 1.0 - amount
    scale = (1.0 / relax_time) * share * density
    base = scale - (1.5 * scale) * (ux * ux + uy * uy + uz * uz)
    curve, slope = 4.5 * scale, 3.0 * scale
    rest = (1.0 / relax_time - 1.0) * share
    even_part, odd_part = 0.5 * (amount - rest), 0.5 * (amount + rest)
    put(0, base + (amount - rest) * f[0])
    along_all = (ux, uy, uz, ux + uy, ux - uy, ux + uz, ux - uz, uy + uz, uy - uz)
    for pair in range(9):
        along = along_all[pair]
        even = base + (curve * along) * along + even_part * pair_sum[pair]
        odd = slope * along - odd_part * pair_dif[pair]
        put(2 * pair + 1, even + odd)
        put(2 * pair + 2, even - odd)


def deal_kernel(front, table, done, fresh, got_mixed, got_base, got_solid, new_pop, new_sol, new_solid, ones, placed, sems):
    copies = []
    for k in range(SLOTS - 3):
        slot = rest_slot(k, front)
        copies.append(pltpu.make_async_copy(done.at[k], new_pop.at[slot], sems.at[0, 3 + k]))
        copies.append(pltpu.make_async_copy(fresh.at[k, 0], new_sol.at[slot], sems.at[1, 3 + k]))
        copies.append(pltpu.make_async_copy(fresh.at[k, 1], new_solid.at[slot], sems.at[2, 3 + k]))
    for copy in copies:
        copy.start()
    ones[...] = jnp.ones(ones.shape, BF16)
    for k in range(3):
        slot = place_slot(k, front, table)
        placed[0, k], placed[1, k] = react(got_base[k] + got_mixed[k].astype(F32), got_solid[k])
        late = [pltpu.make_async_copy(ones, new_pop.at[slot], sems.at[0, k]),
                pltpu.make_async_copy(placed.at[0, k], new_sol.at[slot], sems.at[1, k]),
                pltpu.make_async_copy(placed.at[1, k], new_solid.at[slot], sems.at[2, k])]
        for copy in late:
            copy.start()
        copies += late

    for copy in copies:
        copy.wait()


def deal(front, table, done, fresh, got_mixed, got_base, got_solid):
    smem, vmem, anywhere = (pl.BlockSpec(memory_space=m) for m in (pltpu.SMEM, pltpu.VMEM, pl.ANY))
    return pl.pallas_call(
        deal_kernel,
        out_shape=(
            jax.ShapeDtypeStruct((SLOTS, 19, S, CELLS), BF16),
            jax.ShapeDtypeStruct((SLOTS, S, CELLS), F32),
            jax.ShapeDtypeStruct((SLOTS, S, CELLS), F32),
        ),
        in_specs=[smem] * 2 + [vmem] * 5,
        out_specs=(anywhere,) * 3,
        scratch_shapes=[
            pltpu.VMEM((19, S, CELLS), BF16),
            pltpu.VMEM((2, 3, S, CELLS), F32),
            pltpu.SemaphoreType.DMA((3, SLOTS)),
        ],
        compiler_params=pltpu.CompilerParams(vmem_limit_bytes=8 * 2**20),
        cost_estimate=pl.CostEstimate(flops=10**8, bytes_accessed=16 * 10**6, transcendentals=0),
        name="deal",
    )(front, table, done, fresh, got_mixed, got_base, got_solid)


def body(populations, solute, solid_fraction, neighbours, front_list, redeal_list):
    done, fresh, got_mixed, got_base, got_solid, table = exchange(
        populations, solute, solid_fraction, neighbours, front_list, redeal_list)
    return deal(front_list, table, done, fresh, got_mixed, got_base, got_solid)


def solution(mesh):
    deal = ("blk", "grp")
    return jax.shard_map(
        body,
        mesh=mesh,
        in_specs=(P(deal, None, None, None), P(deal, None, None), P(deal, None, None), P(deal, None), P(deal), P(deal)),
        out_specs=(P(deal, None, None, None), P(deal, None, None), P(deal, None, None)),
        check_vma=False,
    )
```
